32 devices in a mesh: dom: 8 (over z, x), head: 4 (over y, core).
Axes of the slice: x: 2, y: 2, z: 4, core: 2. Of those that a mesh axis runs over, the one named last changes fastest.
Arguments:
- vertex_embeddings: bfloat16 [4096, 512], P(('dom', 'head')), may hold values from -6 to 6
- adjacent_group_bank_ids: int32 [8, 4, 12], P('dom', 'head'), may hold values from -1 to 15, as said below
- coupling_strength_panels: bfloat16 [16, 128, 128], replicated, may hold values from -0.3125 to 0.3125
- asking_projector: bfloat16 [512, 512], replicated, may hold values from -0.25 to 0.25
- lookup_projector: bfloat16 [512, 512], replicated, may hold values from -0.25 to 0.25
- content_projector: bfloat16 [512, 512], replicated, may hold values from -0.25 to 0.25
- final_projector: bfloat16 [512, 512], replicated, may hold values from -0.25 to 0.25
- passing_inner_coefficients: bfloat16 [512, 1024], replicated, may hold values from -0.25 to 0.25
- passing_outer_coefficients: bfloat16 [1024, 512], replicated, may hold values from -0.1875 to 0.1875
- softness_per_subspace: float32 [8], replicated, may hold values from 0.5 to 2
- mixing_layer_gain: float32 [512], replicated, may hold values from 0.5 to 1.5
Outputs:
- result: bfloat16 [4096, 512], P(('dom', 'head'))
The draws below stay inside these ranges and needn't reach their ends.
Inputs may be any that keep to these rules, and one draw needn't show every extreme that they name: `adjacent_group_bank_ids`: -1 marks a block without edges. The entry of a block for itself is never -1, nor is at least one entry for each neighbouring partition.
All inputs are finite; a program needn't handle non-finite values.
Results may differ from the reference program's by a relative error of at most 0.0054.
Values may be sent and summed in bfloat16 or wider, within the bound.
No kernel may reach another device: no remote copies, remote signals or barrier semaphores. Data moves between devices by JAX's collectives and lax.ppermute only.
A program may use at most 64 MiB of HBM per device.

```python
import math
import jax
import jax.numpy as jnp
from jax import lax

D = 512
NUM_SUBSPACES = 8
SUBSPACE_WIDTH = 64
FF = 1024
TILES = 16
NODE_DEV = 128
PART = 512
NODES = 4096
N_DOM = 8
N_HEAD = 4


def draw_adjacent_group_bank_ids(key, part):
    key_listed, key_tile, key_left, key_right = jax.random.split(key, 4)
    shape = (N_DOM, N_HEAD, 3 * N_HEAD)
    listed = jax.random.randint(key_listed, shape, 0, 5) < 2
    tile_ids = jax.random.randint(key_tile, shape, 0, TILES)
    pick_left = jax.random.randint(key_left, (N_DOM, N_HEAD, 1), 0, N_HEAD)
    pick_right = jax.random.randint(key_right, (N_DOM, N_HEAD, 1), 0, N_HEAD)
    slots = jnp.arange(3 * N_HEAD)[None, None, :]
    own_slot = slots == (N_HEAD + jnp.arange(N_HEAD))[None, :, None]
    forced = own_slot | (slots == pick_left) | (slots == 2 * N_HEAD + pick_right)
    return jnp.where(listed | forced, tile_ids, -1).astype(jnp.int32)


def block_levels(own_key, extent, cuts, low, largest):
    def one(dim, parts):
        heights = jax.random.uniform(jax.random.fold_in(jax.random.fold_in(own_key, 6), dim), (parts,), jnp.float32, low / len(cuts), largest / len(cuts))
        return jnp.repeat(jnp.exp(heights), extent[dim] // parts).reshape((-1,) + (1,) * (len(extent) - dim - 1))

    loudness = one(*cuts[0])
    for cut in cuts[1:]:
        loudness = loudness * one(*cut)
    return loudness


def scatter_about(stream_key, extent, width, limit, cuts=(), held_as=jnp.bfloat16):
    values = width * jax.random.normal(stream_key, extent, jnp.float32)
    if cuts:
        values = values * block_levels(stream_key, extent, cuts, -0.22, 0.18)
    return jnp.clip(values, -limit, limit).astype(held_as)


def setup_inputs(seed: int = 0) -> dict:
    key_list = jax.random.split(jax.random.key(seed), 12)
    return {
        "vertex_embeddings": scatter_about(key_list[0], (NODES, D), 1.0, 6.0, ((0, 32),)),
        "adjacent_group_bank_ids": draw_adjacent_group_bank_ids(jax.random.fold_in(key_list[11], 71), 0),
        "coupling_strength_panels": scatter_about(key_list[2], (TILES, NODE_DEV, NODE_DEV), (3 * NODE_DEV) ** -0.5, 0.3125),
        "asking_projector": scatter_about(key_list[3], (D, D), D ** -0.5, 0.25),
        "lookup_projector": scatter_about(key_list[4], (D, D), D ** -0.5, 0.25),
        "content_projector": scatter_about(key_list[5], (D, D), D ** -0.5, 0.25),
        "final_projector": scatter_about(key_list[6], (D, D), D ** -0.5, 0.25),
        "passing_inner_coefficients": scatter_about(key_list[7], (D, FF), D ** -0.5, 0.25),
        "passing_outer_coefficients": scatter_about(key_list[8], (FF, D), FF ** -0.5, 0.1875),
        "softness_per_subspace": jnp.clip(jnp.exp(jax.random.uniform(key_list[9], (NUM_SUBSPACES,), jnp.float32, math.log(0.5), math.log(2.0))), 0.5, 2.0),
        "mixing_layer_gain": jnp.clip(1.0 + 0.1 * jax.random.normal(key_list[10], (D,), jnp.float32), 0.5, 1.5),
    }


norm_eps = 1e-06

def head_norm(projected, scales):
    grouped = projected.reshape(projected.shape[0], NUM_SUBSPACES, SUBSPACE_WIDTH)
    mean_square = lax.optimization_barrier(jnp.mean(grouped * grouped, axis=-1, keepdims=True))
    scaled = grouped * lax.rsqrt(mean_square + norm_eps) * scales
    return scaled.reshape(projected.shape[0], D).astype(jnp.bfloat16)

def reference(vertex_embeddings, adjacent_group_bank_ids, coupling_strength_panels, asking_projector, lookup_projector, content_projector, final_projector, passing_inner_coefficients, passing_outer_coefficients, softness_per_subspace, mixing_layer_gain):
    block_len = NODE_DEV
    blocks = vertex_embeddings.reshape(N_DOM, N_HEAD, block_len, D)
    zero_pad = jnp.zeros((1, N_HEAD, block_len, D), vertex_embeddings.dtype)
    padded = jnp.concatenate([zero_pad, blocks, zero_pad], axis=0)
    link_rows = adjacent_group_bank_ids.reshape(N_DOM * N_HEAD, 3 * N_HEAD)

    def block_message(device_id):
        part_index = (device_id // N_HEAD).astype(jnp.int32)
        nearby = lax.dynamic_slice_in_dim(padded, part_index, 3, 0).reshape(3 * N_HEAD * block_len, D)
        slot_ids = link_rows[device_id]
        selected = jnp.take(coupling_strength_panels, jnp.maximum(slot_ids, 0), axis=0)
        selected = jnp.where((slot_ids >= 0)[:, None, None], selected, jnp.zeros_like(selected))
        wide_tiles = jnp.transpose(selected, (1, 0, 2)).reshape(block_len, 3 * N_HEAD * block_len)
        return jnp.dot(wide_tiles, nearby, preferred_element_type=jnp.float32).astype(jnp.bfloat16)
    aggregate = lax.map(block_message, jnp.arange(N_DOM * N_HEAD, dtype=jnp.int32)).reshape(NODES, D)
    hidden = jax.nn.gelu(jnp.dot(aggregate, passing_inner_coefficients, preferred_element_type=jnp.float32)).astype(jnp.bfloat16)
    local_term = jnp.dot(hidden, passing_outer_coefficients, preferred_element_type=jnp.float32)
    asking_vector_multiplier = (softness_per_subspace / math.sqrt(SUBSPACE_WIDTH))[None, :, None]
    queries = head_norm(jnp.dot(vertex_embeddings, asking_projector, preferred_element_type=jnp.float32), asking_vector_multiplier)
    keys_all = head_norm(jnp.dot(vertex_embeddings, lookup_projector, preferred_element_type=jnp.float32), jnp.ones((1, NUM_SUBSPACES, 1), jnp.float32))
    values_all = jnp.dot(vertex_embeddings, content_projector, preferred_element_type=jnp.float32).astype(jnp.bfloat16)

    def attend(query_block):
        pieces = []
        for head_id in range(NUM_SUBSPACES):
            cols = slice(head_id * SUBSPACE_WIDTH, (head_id + 1) * SUBSPACE_WIDTH)
            scores = jnp.dot(query_block[:, cols], keys_all[:, cols].T, preferred_element_type=jnp.float32)
            weights = jnp.exp(scores).astype(jnp.bfloat16)
            denominator = lax.optimization_barrier(jnp.sum(weights, axis=1, keepdims=True, dtype=jnp.float32))
            numerator = jnp.dot(weights, values_all[:, cols], preferred_element_type=jnp.float32)
            pieces.append((numerator / denominator).astype(jnp.bfloat16))
        return jnp.concatenate(pieces, axis=1)
    mixed = lax.map(attend, queries.reshape(NODES // PART, PART, D)).reshape(NODES, D)
    attended = jnp.dot(mixed, final_projector, preferred_element_type=jnp.float32)
    normed = attended * lax.rsqrt(lax.optimization_barrier(jnp.mean(attended * attended, axis=-1, keepdims=True)) + norm_eps) * mixing_layer_gain
    return (vertex_embeddings.astype(jnp.float32) + local_term + normed).astype(jnp.bfloat16)
```

```python
import math

import jax
import jax.numpy as jnp
from jax import lax
from jax.experimental import pallas as pl
from jax.experimental.pallas import tpu as pltpu
from jax.sharding import PartitionSpec as P

NUM_SUBSPACES = 8
SUBSPACE_WIDTH = 64
PAIRS = NUM_SUBSPACES // 2
LANES = 128
norm_eps = 1e-06
VMEM = pl.BlockSpec(memory_space=pltpu.VMEM)
SMEM = pl.BlockSpec(memory_space=pltpu.SMEM)
F32 = jnp.float32
BF16 = jnp.bfloat16
VMEM_LIMIT = 48 * 1024 * 1024


def params():
    return pltpu.CompilerParams(vmem_limit_bytes=VMEM_LIMIT)


def cost(flops, transcendentals, data):
    return pl.CostEstimate(flops=flops, transcendentals=transcendentals, bytes_accessed=data)


def swap(array, axis, mask):
    devices = lax.axis_size(axis)
    return lax.ppermute(array, axis, [(i, i ^ mask) for i in range(devices)])


def swap_both(array, dom_mask, head_mask):
    doms, heads = lax.axis_size("dom"), lax.axis_size("head")
    pairs = [
        (d * heads + h, (d ^ dom_mask) * heads + (h ^ head_mask))
        for d in range(doms)
        for h in range(heads)
    ]
    return lax.ppermute(array, ("dom", "head"), pairs)


def dot(a, b):
    return jnp.dot(a, b, preferred_element_type=F32)


def dot_t(a, b):
    return lax.dot_general(a, b, (((1,), (1,)), ((), ())), preferred_element_type=F32)


def same_head(rows, cols, value):
    row = lax.broadcasted_iota(jnp.int32, (rows, cols), 0) // SUBSPACE_WIDTH
    col = lax.broadcasted_iota(jnp.int32, (rows, cols), 1) // SUBSPACE_WIDTH
    return jnp.where(row == col, value, 0.0).astype(BF16)


def head_normed(projected):
    block = same_head(256, 256, 1.0 / SUBSPACE_WIDTH)
    squares = (projected * projected).astype(BF16)
    mean = jnp.concatenate(
        [dot(squares[:, i : i + 256], block) for i in range(0, projected.shape[1], 256)], axis=1
    )
    return projected * lax.rsqrt(mean + norm_eps)


def padded_queries(queries, pair):
    both = queries[:, pair * LANES : (pair + 1) * LANES]
    first = lax.broadcasted_iota(jnp.int32, both.shape, 1) < SUBSPACE_WIDTH
    zero = jnp.zeros_like(both)
    return jnp.concatenate([jnp.where(first, both, zero), jnp.where(first, zero, both)], axis=0)


def attend(queries, keys_ref, values_ref):
    rows = queries.shape[0]
    count = keys_ref.shape[0]
    ones = jnp.ones((count, LANES), BF16)
    numer, denom = [], []
    first = lax.broadcasted_iota(jnp.int32, (rows, LANES), 1) < SUBSPACE_WIDTH
    for pair in range(PAIRS):
        cols = slice(pair * LANES, (pair + 1) * LANES)
        scores = dot_t(padded_queries(queries, pair), keys_ref[:, cols])
        weights = jnp.exp2(scores).astype(BF16)
        sums = dot(weights, jnp.concatenate([values_ref[:, cols], ones], axis=1))
        numer.append(jnp.where(first, sums[:rows, :LANES], sums[rows:, :LANES]))
        denom.append(jnp.where(first, sums[:rows, LANES:], sums[rows:, LANES:]))
    return jnp.concatenate(numer, axis=1), jnp.concatenate(denom, axis=1)


def keys_values(blocks, lookup_ref, content_ref, keys_ref, values_ref):
    nodes = jnp.concatenate([block[...] for block in blocks], axis=0)
    keys_ref[...] = head_normed(dot(nodes, lookup_ref[...])).astype(BF16)
    values_ref[...] = dot(nodes, content_ref[...]).astype(BF16)


def near_kernel(softness_ref, mine_ref, other_ref, *refs):
    blocks, (asking_ref, lookup_ref, content_ref) = refs[:8], refs[8:11]
    queries_ref, numer_ref, denom_ref, keys_ref, values_ref = refs[11:]
    width = asking_ref.shape[1]
    head = lax.broadcasted_iota(jnp.int32, (1, width), 1) // SUBSPACE_WIDTH
    scale = jnp.zeros((1, width), F32)
    for h in range(NUM_SUBSPACES):
        scale = jnp.where(head == h, softness_ref[h], scale)
    scale = scale * (math.log2(math.e) / math.sqrt(SUBSPACE_WIDTH))
    rows = jnp.concatenate([mine_ref[...], other_ref[...]], axis=0)
    queries = (head_normed(dot(rows, asking_ref[...])) * scale).astype(BF16)
    queries_ref[...] = queries
    keys_values(blocks, lookup_ref, content_ref, keys_ref, values_ref)
    numer_ref[...], denom_ref[...] = attend(queries, keys_ref, values_ref)


def near(softness, mine, other, blocks, asking, lookup, content):
    rows, width = 2 * mine.shape[0], mine.shape[1]
    count = len(blocks) * mine.shape[0]
    return pl.pallas_call(
        near_kernel,
        out_shape=(
            jax.ShapeDtypeStruct((rows, width), BF16),
            jax.ShapeDtypeStruct((rows, width), F32),
            jax.ShapeDtypeStruct((rows, width), F32),
        ),
        in_specs=[SMEM] + [VMEM] * 13,
        out_specs=(VMEM,) * 3,
        scratch_shapes=[pltpu.VMEM((count, width), BF16)] * 2,
        compiler_params=params(),
        cost_estimate=cost(8 * rows * count * width, rows * count * NUM_SUBSPACES, 4 << 20),
        name="near",
    )(softness, mine, other, *blocks, asking, lookup, content)


def packing(width, wide):
    lane = lax.broadcasted_iota(jnp.int32, (width, LANES), 1)
    col = lax.broadcasted_iota(jnp.int32, (width, LANES), 0)
    if wide:
        return lane, col // SUBSPACE_WIDTH
    return lane * SUBSPACE_WIDTH, col


def pack(numer, denom):
    width = numer.shape[1]
    high = denom.astype(BF16)
    low = (denom - high.astype(F32)).astype(BF16)
    lane, col = packing(width, False)
    to_high = jnp.where((lane == col), 1.0, 0.0).astype(BF16)
    to_low = jnp.where((lane == col + width), 1.0, 0.0).astype(BF16)
    sums = dot(high, to_high) + dot(low, to_low)
    return jnp.concatenate([numer.astype(BF16), sums.astype(BF16)], axis=1)


def unpack_denom(packed, width):
    lane, head = packing(width, True)
    spread = ((lane == head) | (lane == head + NUM_SUBSPACES)) & (lane < 2 * NUM_SUBSPACES)
    return dot_t(packed, jnp.where(spread, 1.0, 0.0).astype(BF16))


def far_kernel(*refs):
    blocks, (lookup_ref, content_ref, queries_ref, numer_ref, denom_ref) = refs[:8], refs[8:13]
    keys_ref, values_ref, packed_ref, numer_sum, denom_sum = refs[13:]
    step = pl.program_id(0)
    half = queries_ref.shape[0] // 2

    @pl.when(step == 0)
    def _():
        numer_sum[...] = numer_ref[half:, :]
        denom_sum[...] = denom_ref[half:, :]

    keys_values(blocks, lookup_ref, content_ref, keys_ref, values_ref)
    numer, denom = attend(queries_ref[half:, :], keys_ref, values_ref)
    numer_sum[...] += numer
    denom_sum[...] += denom

    @pl.when(step == pl.num_programs(0) - 1)
    def _():
        packed_ref[...] = pack(numer_sum[...], denom_sum[...])


def far(blocks, block_len, lookup, content, queries, numer, denom):
    steps = blocks[0].shape[0] // block_len
    rows, width = queries.shape
    half = rows // 2
    count = len(blocks) * block_len
    whole = lambda shape: pl.BlockSpec(shape, lambda i: (0, 0))
    part = lambda size: pl.BlockSpec((size, width), lambda i: (i, 0))
    return pl.pallas_call(
        far_kernel,
        grid=(steps,),
        out_shape=(
            jax.ShapeDtypeStruct((steps * count, width), BF16),
            jax.ShapeDtypeStruct((steps * count, width), BF16),
            jax.ShapeDtypeStruct((half, width + LANES), BF16),
        ),
        in_specs=[part(block_len)] * 8
        + [whole((width, width))] * 2
        + [whole((rows, width))] * 3,
        out_specs=(part(count), part(count), whole((half, width + LANES))),
        scratch_shapes=[pltpu.VMEM((half, width), F32)] * 2,
        compiler_params=params(),
        cost_estimate=cost(
            6 * half * steps * count * width, half * steps * count * NUM_SUBSPACES, 4 << 20
        ),
        name="far",
    )(*blocks, lookup, content, queries, numer, denom)


def own_kernel(keys_ref, values_ref, queries_ref, numer_ref, denom_ref, numer_out, denom_out):
    half = queries_ref.shape[0] // 2

    @pl.when(pl.program_id(0) == 0)
    def _():
        numer_out[...] = numer_ref[:half, :]
        denom_out[...] = denom_ref[:half, :]

    numer, denom = attend(queries_ref[:half, :], keys_ref, values_ref)
    numer_out[...] += numer
    denom_out[...] += denom


def own(keys, values, count, queries, numer, denom):
    steps = keys.shape[0] // count
    rows, width = queries.shape
    half = rows // 2
    whole = lambda shape: pl.BlockSpec(shape, lambda i: (0, 0))
    part = lambda size: pl.BlockSpec((size, width), lambda i: (i, 0))
    return pl.pallas_call(
        own_kernel,
        grid=(steps,),
        out_shape=(jax.ShapeDtypeStruct((half, width), F32),) * 2,
        in_specs=[part(count)] * 2 + [whole((rows, width))] * 3,
        out_specs=(whole((half, width)),) * 2,
        compiler_params=params(),
        cost_estimate=cost(
            4 * half * steps * count * width, half * steps * count * NUM_SUBSPACES, 4 << 20
        ),
        name="own",
    )(keys, values, queries, numer, denom)


def message_kernel(slots_ref, place_ref, tiles_ref, *refs):
    blocks, (inner_ref, outer_ref, local_ref) = refs[:12], refs[12:]
    group = slots_ref.shape[0] // 3
    me, odd = place_ref[0], place_ref[1]
    sides = (1, 2 - 2 * odd, 2 * odd)
    tiles = []
    for i in range(12):
        tile_id = slots_ref[sides[i // 4] * group + (me ^ (i % 4))]
        tile = tiles_ref[jnp.maximum(tile_id, 0)]
        tiles.append(jnp.where(tile_id >= 0, tile, jnp.zeros_like(tile)))
    nodes = jnp.concatenate([block[...] for block in blocks], axis=0)
    aggregate = dot(jnp.concatenate(tiles, axis=1), nodes).astype(BF16)
    hidden = jax.nn.gelu(dot(aggregate, inner_ref[...])).astype(BF16)
    local_ref[...] = dot(hidden, outer_ref[...])


def message(slots, place, tiles, blocks, inner, outer):
    rows, width = blocks[0].shape
    hidden = inner.shape[1]
    return pl.pallas_call(
        message_kernel,
        out_shape=jax.ShapeDtypeStruct((rows, width), F32),
        in_specs=[SMEM, SMEM] + [VMEM] * 15,
        out_specs=VMEM,
        compiler_params=params(),
        cost_estimate=cost(
            2 * rows * width * (12 * rows + 2 * hidden), rows * hidden, 4 << 20
        ),
        name="message",
    )(slots, place, tiles, *blocks, inner, outer)


def finish_kernel(
    numer_ref, denom_ref, packed_ref, final_ref, gain_ref, local_ref, nodes_ref, out_ref
):
    width = numer_ref.shape[1]
    numer = numer_ref[...] + packed_ref[:, :width].astype(F32)
    denom = denom_ref[...] + unpack_denom(packed_ref[:, width:], width)
    mixed = (numer / denom).astype(BF16)
    attended = dot(mixed, final_ref[...])
    mean = jnp.mean(attended * attended, axis=-1, keepdims=True)
    normed = attended * lax.rsqrt(mean + norm_eps) * gain_ref[...]
    out_ref[...] = (nodes_ref[...].astype(F32) + local_ref[...] + normed).astype(BF16)


def finish(numer, denom, packed, final, gain, local, nodes):
    rows, width = nodes.shape
    return pl.pallas_call(
        finish_kernel,
        out_shape=jax.ShapeDtypeStruct((rows, width), BF16),
        in_specs=[VMEM] * 7,
        out_specs=VMEM,
        compiler_params=params(),
        cost_estimate=cost(2 * rows * width * width, rows, 2 << 20),
        name="finish",
    )(numer, denom, packed, final, gain, local, nodes)


def shards(
    vertex_embeddings,
    adjacent_group_bank_ids,
    coupling_strength_panels,
    asking_projector,
    lookup_projector,
    content_projector,
    final_projector,
    passing_inner_coefficients,
    passing_outer_coefficients,
    softness_per_subspace,
    mixing_layer_gain,
):
    block_len = vertex_embeddings.shape[0]
    doms = lax.axis_size("dom")
    nodes = vertex_embeddings

    distant = nodes[:0]
    mask = 4
    while mask < doms:
        held = jnp.concatenate([nodes, distant], axis=0) if mask > 4 else nodes
        arrived = swap(held, "dom", mask)
        distant = jnp.concatenate([distant, arrived], axis=0) if mask > 4 else arrived
        mask *= 2

    def plane(block):
        side = swap(block, "dom", 1)
        below = swap(block, "head", 2)
        across = swap_both(block, 1, 2)
        return block, below, side, across

    others = swap(nodes, "dom", 2)
    near_blocks = plane(nodes)
    near_twins = [swap(block, "head", 1) for block in near_blocks]
    pairs = [(p, p + 2) for p in range(0, doms - 2, 2)] + [(p, p - 2) for p in range(3, doms, 2)]
    halo = [lax.ppermute(block, "dom", pairs) for block in near_blocks[2:]]
    halo_twins = [swap(block, "head", 1) for block in halo]
    far_blocks = plane(distant)
    far_twins = [swap(block, "head", 1) for block in far_blocks]

    interleave = lambda a, b: [block for both in zip(a, b) for block in both]
    queries, numer, denom = near(
        softness_per_subspace,
        nodes,
        others,
        interleave(near_blocks, near_twins),
        asking_projector,
        lookup_projector,
        content_projector,
    )
    place = jnp.stack([lax.axis_index("head"), lax.axis_index("dom") % 2]).astype(jnp.int32)
    local = message(
        adjacent_group_bank_ids.reshape(-1),
        place,
        coupling_strength_panels,
        interleave(near_blocks, near_twins) + interleave(halo, halo_twins),
        passing_inner_coefficients,
        passing_outer_coefficients,
    )
    keys, values, packed = far(
        interleave(far_blocks, far_twins),
        block_len,
        lookup_projector,
        content_projector,
        queries,
        numer,
        denom,
    )
    packed = swap(packed, "dom", 2)
    numer, denom = own(keys, values, 8 * block_len, queries, numer, denom)
    return finish(
        numer,
        denom,
        packed,
        final_projector,
        mixing_layer_gain.reshape(1, -1),
        local,
        nodes,
    )


def solution(mesh):
    in_specs = (P(("dom", "head"), None), P("dom", "head", None)) + (P(),) * 9
    out_specs = P(("dom", "head"), None)
    return jax.shard_map(shards, mesh=mesh, in_specs=in_specs, out_specs=out_specs, check_vma=False)
```

```python
import math

import jax
import jax.numpy as jnp
from jax import lax
from jax.experimental import pallas as pl
from jax.experimental.pallas import tpu as pltpu
from jax.sharding import PartitionSpec as P

NUM_SUBSPACES = 8
SUBSPACE_WIDTH = 64
PAIRS = NUM_SUBSPACES // 2
LANES = 128
norm_eps = 1e-06
VMEM = pl.BlockSpec(memory_space=pltpu.VMEM)
SMEM = pl.BlockSpec(memory_space=pltpu.SMEM)
ANY = pl.BlockSpec(memory_space=pl.ANY)
F32 = jnp.float32
BF16 = jnp.bfloat16
VMEM_LIMIT = 48 * 1024 * 1024


def params():
    return pltpu.CompilerParams(vmem_limit_bytes=VMEM_LIMIT)


def cost(flops, transcendentals, data):
    return pl.CostEstimate(flops=flops, transcendentals=transcendentals, bytes_accessed=data)


def swap(array, axis, mask):
    devices = lax.axis_size(axis)
    return lax.ppermute(array, axis, [(i, i ^ mask) for i in range(devices)])


def swap_both(array, dom_mask, head_mask):
    doms, heads = lax.axis_size("dom"), lax.axis_size("head")
    pairs = [
        (d * heads + h, (d ^ dom_mask) * heads + (h ^ head_mask))
        for d in range(doms)
        for h in range(heads)
    ]
    return lax.ppermute(array, ("dom", "head"), pairs)


def dot(a, b):
    return jnp.dot(a, b, preferred_element_type=F32)


def dot_t(a, b):
    return lax.dot_general(a, b, (((1,), (1,)), ((), ())), preferred_element_type=F32)


def same_head(rows, cols, value):
    row = lax.broadcasted_iota(jnp.int32, (rows, cols), 0) // SUBSPACE_WIDTH
    col = lax.broadcasted_iota(jnp.int32, (rows, cols), 1) // SUBSPACE_WIDTH
    return jnp.where(row == col, value, 0.0).astype(BF16)


def head_normed(projected):
    block = same_head(256, 256, 1.0 / SUBSPACE_WIDTH)
    squares = (projected * projected).astype(BF16)
    mean = jnp.concatenate(
        [dot(squares[:, i : i + 256], block) for i in range(0, projected.shape[1], 256)], axis=1
    )
    return projected * lax.rsqrt(mean + norm_eps)


def padded_queries(queries, pair):
    both = queries[:, pair * LANES : (pair + 1) * LANES]
    first = lax.broadcasted_iota(jnp.int32, both.shape, 1) < SUBSPACE_WIDTH
    zero = jnp.zeros_like(both)
    return jnp.concatenate([jnp.where(first, both, zero), jnp.where(first, zero, both)], axis=0)


def attend(queries, keys_ref, values_ref):
    rows = queries.shape[0]
    count = keys_ref.shape[0]
    ones = jnp.ones((count, LANES), BF16)
    numer, denom = [], []
    first = lax.broadcasted_iota(jnp.int32, (rows, LANES), 1) < SUBSPACE_WIDTH
    for pair in range(PAIRS):
        cols = slice(pair * LANES, (pair + 1) * LANES)
        scores = dot_t(padded_queries(queries, pair), keys_ref[:, cols])
        weights = jnp.exp2(scores).astype(BF16)
        sums = dot(weights, jnp.concatenate([values_ref[:, cols], ones], axis=1))
        numer.append(jnp.where(first, sums[:rows, :LANES], sums[rows:, :LANES]))
        denom.append(jnp.where(first, sums[:rows, LANES:], sums[rows:, LANES:]))
    return jnp.concatenate(numer, axis=1), jnp.concatenate(denom, axis=1)


def keys_values(blocks, lookup_ref, content_ref, keys_ref, values_ref):
    nodes = jnp.concatenate([block[...] for block in blocks], axis=0)
    keys_ref[...] = head_normed(dot(nodes, lookup_ref[...])).astype(BF16)
    values_ref[...] = dot(nodes, content_ref[...]).astype(BF16)


def prep_kernel(*refs):
    count = (len(refs) - 1) // 2
    sources, targets, sems = refs[:count], refs[count:-1], refs[-1]
    copies = [
        pltpu.make_async_copy(source, target, sems.at[i])
        for i, (source, target) in enumerate(zip(sources, targets))
    ]
    for copy in copies:
        copy.start()
    for copy in copies:
        copy.wait()


def prep(*arrays):
    return pl.pallas_call(
        prep_kernel,
        out_shape=tuple(jax.ShapeDtypeStruct(a.shape, a.dtype) for a in arrays),
        in_specs=[ANY] * len(arrays),
        out_specs=(VMEM,) * len(arrays),
        scratch_shapes=[pltpu.SemaphoreType.DMA((len(arrays),))],
        compiler_params=params(),
        cost_estimate=cost(0, 0, 9 << 20),
        name="prep",
    )(*arrays)


def near_kernel(softness_ref, mine_ref, other_ref, twins_ref, *refs):
    blocks, (asking_ref, lookup_ref, content_ref) = refs[:3], refs[3:6]
    queries_ref, numer_ref, denom_ref, keys_ref, values_ref, temper, sem = refs[6:]
    copy = pltpu.make_async_copy(softness_ref, temper, sem)
    copy.start()
    keys_values((mine_ref,) + blocks, lookup_ref, content_ref, keys_ref, values_ref)
    rows = jnp.concatenate([twins_ref[...], mine_ref[...], other_ref[...]], axis=0)
    projected = head_normed(dot(rows, asking_ref[...]))
    copy.wait()
    width = asking_ref.shape[1]
    head = lax.broadcasted_iota(jnp.int32, (1, width), 1) // SUBSPACE_WIDTH
    scale = jnp.zeros((1, width), F32)
    for h in range(NUM_SUBSPACES):
        scale = jnp.where(head == h, temper[h], scale)
    scale = scale * (math.log2(math.e) / math.sqrt(SUBSPACE_WIDTH))
    queries = (projected * scale).astype(BF16)
    queries_ref[...] = queries
    numer_ref[...], denom_ref[...] = attend(queries, keys_ref, values_ref)


def near(softness, mine, other, twins, blocks, asking, lookup, content):
    rows, width = 4 * mine.shape[0], mine.shape[1]
    count = 4 * mine.shape[0]
    return pl.pallas_call(
        near_kernel,
        out_shape=(
            jax.ShapeDtypeStruct((rows, width), BF16),
            jax.ShapeDtypeStruct((rows, width), F32),
            jax.ShapeDtypeStruct((rows, width), F32),
        ),
        in_specs=[ANY] + [VMEM] * 9,
        out_specs=(VMEM,) * 3,
        scratch_shapes=[pltpu.VMEM((count, width), BF16)] * 2
        + [pltpu.SMEM(softness.shape, F32), pltpu.SemaphoreType.DMA],
        compiler_params=params(),
        cost_estimate=cost(8 * rows * count * width, rows * count * NUM_SUBSPACES, 4 << 20),
        name="near",
    )(softness, mine, other, twins, *blocks, asking, lookup, content)


def packing(width, wide):
    lane = lax.broadcasted_iota(jnp.int32, (width, LANES), 1)
    col = lax.broadcasted_iota(jnp.int32, (width, LANES), 0)
    if wide:
        return lane, col // SUBSPACE_WIDTH
    return lane * SUBSPACE_WIDTH, col


def pack(numer, denom):
    width = numer.shape[1]
    high = denom.astype(BF16)
    low = (denom - high.astype(F32)).astype(BF16)
    lane, col = packing(width, False)
    to_high = jnp.where((lane == col), 1.0, 0.0).astype(BF16)
    to_low = jnp.where((lane == col + width), 1.0, 0.0).astype(BF16)
    sums = dot(high, to_high) + dot(low, to_low)
    return jnp.concatenate([numer.astype(BF16), sums.astype(BF16)], axis=1)


def unpack_denom(packed, width):
    lane, head = packing(width, True)
    spread = ((lane == head) | (lane == head + NUM_SUBSPACES)) & (lane < 2 * NUM_SUBSPACES)
    return dot_t(packed, jnp.where(spread, 1.0, 0.0).astype(BF16))


def far_kernel(*refs):
    blocks, (lookup_ref, content_ref, queries_ref, numer_ref, denom_ref) = refs[:4], refs[4:9]
    keys_ref, values_ref, packed_ref, numer_sum, denom_sum = refs[9:]
    half = queries_ref.shape[0] // 2
    step = pl.program_id(0)

    @pl.when(step == 0)
    def _():
        numer_sum[...] = numer_ref[:half, :]
        denom_sum[...] = denom_ref[:half, :]

    keys_values(blocks, lookup_ref, content_ref, keys_ref, values_ref)
    numer, denom = attend(queries_ref[:half, :], keys_ref, values_ref)
    numer_sum[...] += numer
    denom_sum[...] += denom

    @pl.when(step == pl.num_programs(0) - 1)
    def _():
        packed_ref[...] = pack(numer_sum[...], denom_sum[...])


def far(blocks, block_len, lookup, content, queries, numer, denom):
    steps = blocks[0].shape[0] // block_len
    rows, width = queries.shape
    half = rows // 2
    count = len(blocks) * block_len
    whole = lambda shape: pl.BlockSpec(shape, lambda i: (0, 0))
    part = lambda size: pl.BlockSpec((size, width), lambda i: (i, 0))
    return pl.pallas_call(
        far_kernel,
        grid=(steps,),
        out_shape=(
            jax.ShapeDtypeStruct((steps * count, width), BF16),
            jax.ShapeDtypeStruct((steps * count, width), BF16),
            jax.ShapeDtypeStruct((half, width + LANES), BF16),
        ),
        in_specs=[part(block_len)] * 4
        + [whole((width, width))] * 2
        + [whole((rows, width))] * 3,
        out_specs=(part(count), part(count), whole((half, width + LANES))),
        scratch_shapes=[pltpu.VMEM((half, width), F32)] * 2,
        compiler_params=params(),
        cost_estimate=cost(
            6 * half * steps * count * width, half * steps * count * NUM_SUBSPACES, 4 << 20
        ),
        name="far",
    )(*blocks, lookup, content, queries, numer, denom)


def rest_kernel(keys_ref, values_ref, queries_ref, numer_ref, denom_ref, numer_out, denom_out):
    half = queries_ref.shape[0] // 2

    @pl.when(pl.program_id(0) == 0)
    def _():
        numer_out[...] = numer_ref[half:, :]
        denom_out[...] = denom_ref[half:, :]

    numer, denom = attend(queries_ref[half:, :], keys_ref, values_ref)
    numer_out[...] += numer
    denom_out[...] += denom


def rest(keys, values, count, queries, numer, denom):
    steps = keys.shape[0] // count
    rows, width = queries.shape
    half = rows // 2
    whole = lambda shape: pl.BlockSpec(shape, lambda i: (0, 0))
    part = lambda size: pl.BlockSpec((size, width), lambda i: (i, 0))
    return pl.pallas_call(
        rest_kernel,
        grid=(steps,),
        out_shape=(jax.ShapeDtypeStruct((half, width), F32),) * 2,
        in_specs=[part(count)] * 2 + [whole((rows, width))] * 3,
        out_specs=(whole((half, width)),) * 2,
        compiler_params=params(),
        cost_estimate=cost(
            4 * half * steps * count * width, half * steps * count * NUM_SUBSPACES, 4 << 20
        ),
        name="rest",
    )(keys, values, queries, numer, denom)


def combine_kernel(numer_ref, denom_ref, packed_ref, numer_out, denom_out, packed_out):
    rows, width = numer_out.shape
    numer = numer_ref[...] + packed_ref[:, :width].astype(F32)
    denom = denom_ref[...] + unpack_denom(packed_ref[:, width:], width)
    numer_out[...] = numer[:rows]
    denom_out[...] = denom[:rows]
    packed_out[...] = pack(numer[rows:], denom[rows:])


def combine(numer, denom, packed):
    rows, width = numer.shape[0] // 2, numer.shape[1]
    return pl.pallas_call(
        combine_kernel,
        out_shape=(
            jax.ShapeDtypeStruct((rows, width), F32),
            jax.ShapeDtypeStruct((rows, width), F32),
            jax.ShapeDtypeStruct((rows, width + LANES), BF16),
        ),
        in_specs=[VMEM] * 3,
        out_specs=(VMEM,) * 3,
        compiler_params=params(),
        cost_estimate=cost(4 * rows * width * LANES, 0, 1 << 20),
        name="combine",
    )(numer, denom, packed)


def message_kernel(slots_ref, place_ref, tiles_ref, *refs):
    blocks, (inner_ref, outer_ref, local_ref, slots, sem) = refs[:7], refs[7:]
    copy = pltpu.make_async_copy(slots_ref, slots, sem)
    copy.start()
    group = slots_ref.shape[0] // 3
    me, odd = place_ref[0], place_ref[1]
    beside, beyond = 2 - 2 * odd, 2 * odd
    order = [(1, 0), (1, 1), (1, 2), (beside, 0), (beside, 2), (beyond, 0), (beyond, 2)]
    order += [(1, 3), (beside, 1), (beside, 3), (beyond, 1), (beyond, 3)]
    copy.wait()
    tiles = []
    for side, offset in order:
        tile_id = slots[side * group + (me ^ offset)]
        tile = tiles_ref[jnp.maximum(tile_id, 0)]
        tiles.append(jnp.where(tile_id >= 0, tile, jnp.zeros_like(tile)))
    nodes = jnp.concatenate([block[...] for block in blocks], axis=0)
    aggregate = dot(jnp.concatenate(tiles, axis=1), nodes).astype(BF16)
    hidden = jax.nn.gelu(dot(aggregate, inner_ref[...])).astype(BF16)
    local_ref[...] = dot(hidden, outer_ref[...])


def message(slots, place, tiles, blocks, inner, outer):
    rows, width = blocks[0].shape
    hidden = inner.shape[1]
    return pl.pallas_call(
        message_kernel,
        out_shape=jax.ShapeDtypeStruct((rows, width), F32),
        in_specs=[ANY, SMEM] + [VMEM] * 10,
        out_specs=VMEM,
        scratch_shapes=[pltpu.SMEM(slots.shape, jnp.int32), pltpu.SemaphoreType.DMA],
        compiler_params=params(),
        cost_estimate=cost(
            2 * rows * width * (12 * rows + 2 * hidden), rows * hidden, 4 << 20
        ),
        name="message",
    )(slots, place, tiles, *blocks, inner, outer)


def finish_kernel(
    numer_ref, denom_ref, packed_ref, final_ref, gain_ref, local_ref, nodes_ref, out_ref
):
    width = numer_ref.shape[1]
    numer = numer_ref[...] + packed_ref[:, :width].astype(F32)
    denom = denom_ref[...] + unpack_denom(packed_ref[:, width:], width)
    mixed = (numer / denom).astype(BF16)
    attended = dot(mixed, final_ref[...])
    mean = jnp.mean(attended * attended, axis=-1, keepdims=True)
    normed = attended * lax.rsqrt(mean + norm_eps) * gain_ref[...]
    out_ref[...] = (nodes_ref[...].astype(F32) + local_ref[...] + normed).astype(BF16)


def finish(numer, denom, packed, final, gain, local, nodes):
    rows, width = nodes.shape
    return pl.pallas_call(
        finish_kernel,
        out_shape=jax.ShapeDtypeStruct((rows, width), BF16),
        in_specs=[VMEM] * 7,
        out_specs=VMEM,
        compiler_params=params(),
        cost_estimate=cost(2 * rows * width * width, rows, 2 << 20),
        name="finish",
    )(numer, denom, packed, final, gain, local, nodes)


def shards(
    vertex_embeddings,
    adjacent_group_bank_ids,
    coupling_strength_panels,
    asking_projector,
    lookup_projector,
    content_projector,
    final_projector,
    passing_inner_coefficients,
    passing_outer_coefficients,
    softness_per_subspace,
    mixing_layer_gain,
):
    block_len = vertex_embeddings.shape[0]
    doms = lax.axis_size("dom")
    nodes = vertex_embeddings
    stacked = lambda *arrays: jnp.concatenate(arrays, axis=0)

    distant = swap(nodes, "dom", 4)
    mask = 8
    while mask < doms:
        distant = stacked(distant, swap(stacked(nodes, distant), "dom", mask))
        mask *= 2

    def plane(block):
        side = swap(block, "dom", 1)
        below = swap(block, "head", 2)
        across = swap_both(block, 1, 2)
        return below, side, across

    near_blocks = plane(nodes)
    other = swap(nodes, "dom", 2)
    twins = swap(stacked(nodes, other), "head", 1)
    far_blocks = (distant,) + plane(distant)

    (
        asking,
        lookup,
        content,
        final,
        inner,
        outer,
        tiles,
        gain,
    ) = prep(
        asking_projector,
        lookup_projector,
        content_projector,
        final_projector,
        passing_inner_coefficients,
        passing_outer_coefficients,
        coupling_strength_panels,
        mixing_layer_gain.reshape(1, -1),
    )
    queries, numer, denom = near(
        softness_per_subspace, nodes, other, twins, near_blocks, asking, lookup, content
    )

    below, side, across = near_blocks
    pairs = [(p, p + 2) for p in range(0, doms - 2, 2)] + [(p, p - 2) for p in range(3, doms, 2)]
    halo = lax.ppermute(stacked(side, across), "dom", pairs)
    halo_twins = swap(stacked(below, side, across, halo), "head", 1)
    place = jnp.stack([lax.axis_index("head"), lax.axis_index("dom") % 2]).astype(jnp.int32)
    local = message(
        adjacent_group_bank_ids.reshape(-1),
        place,
        tiles,
        (nodes, twins[:block_len], below, side, across, halo, halo_twins),
        inner,
        outer,
    )
    keys, values, packed = far(far_blocks, block_len, lookup, content, queries, numer, denom)
    packed = swap(packed, "head", 1)
    numer, denom = rest(keys, values, 4 * block_len, queries, numer, denom)
    numer, denom, packed = combine(numer, denom, packed)
    packed = swap(packed, "dom", 2)
    return finish(numer, denom, packed, final, gain, local, nodes)


def solution(mesh):
    in_specs = (P(("dom", "head"), None), P("dom", "head", None)) + (P(),) * 9
    out_specs = P(("dom", "head"), None)
    return jax.shard_map(shards, mesh=mesh, in_specs=in_specs, out_specs=out_specs, check_vma=False)
```

```python
import functools
import math

import jax
import jax.numpy as jnp
from jax import lax
from jax.experimental import pallas as pl
from jax.experimental.pallas import tpu as pltpu
from jax.sharding import PartitionSpec as P

NUM_SUBSPACES = 8
SUBSPACE_WIDTH = 64
PAIRS = NUM_SUBSPACES // 2
LANES = 128
norm_eps = 1e-06
VMEM = pl.BlockSpec(memory_space=pltpu.VMEM)
ANY = pl.BlockSpec(memory_space=pl.ANY)
F32 = jnp.float32
BF16 = jnp.bfloat16


def params(mebibytes):
    return pltpu.CompilerParams(vmem_limit_bytes=mebibytes << 20)


def cost(flops, transcendentals, data):
    return pl.CostEstimate(
        flops=flops // 16, transcendentals=transcendentals // 16, bytes_accessed=data // 16
    )


def swap(array, axis, mask):
    devices = lax.axis_size(axis)
    return lax.ppermute(array, axis, [(i, i ^ mask) for i in range(devices)])


def swap_both(array, dom_mask, head_mask):
    doms, heads = lax.axis_size("dom"), lax.axis_size("head")
    pairs = [
        (d * heads + h, (d ^ dom_mask) * heads + (h ^ head_mask))
        for d in range(doms)
        for h in range(heads)
    ]
    return lax.ppermute(array, ("dom", "head"), pairs)


def dot(a, b):
    return jnp.dot(a, b, preferred_element_type=F32)


def dot_t(a, b):
    return lax.dot_general(a, b, (((1,), (1,)), ((), ())), preferred_element_type=F32)


def same_head(rows, cols, value):
    row = lax.broadcasted_iota(jnp.int32, (rows, cols), 0) // SUBSPACE_WIDTH
    col = lax.broadcasted_iota(jnp.int32, (rows, cols), 1) // SUBSPACE_WIDTH
    return jnp.where(row == col, value, 0.0).astype(BF16)


def head_normed(projected):
    block = same_head(256, 256, 1.0 / SUBSPACE_WIDTH)
    squares = (projected * projected).astype(BF16)
    mean = jnp.concatenate(
        [dot(squares[:, i : i + 256], block) for i in range(0, projected.shape[1], 256)], axis=1
    )
    return projected * lax.rsqrt(mean + norm_eps)


def padded_queries(queries, pair):
    both = queries[:, pair * LANES : (pair + 1) * LANES]
    first = lax.broadcasted_iota(jnp.int32, both.shape, 1) < SUBSPACE_WIDTH
    zero = jnp.zeros_like(both)
    return jnp.concatenate([jnp.where(first, both, zero), jnp.where(first, zero, both)], axis=0)


def attend(queries, keys_ref, values_ref):
    rows = queries.shape[0]
    count = keys_ref.shape[0]
    ones = jnp.ones((count, LANES), BF16)
    numer, denom = [], []
    first = lax.broadcasted_iota(jnp.int32, (rows, LANES), 1) < SUBSPACE_WIDTH
    for pair in range(PAIRS):
        cols = slice(pair * LANES, (pair + 1) * LANES)
        scores = dot_t(padded_queries(queries, pair), keys_ref[:, cols])
        weights = jnp.exp2(scores).astype(BF16)
        sums = dot(weights, jnp.concatenate([values_ref[:, cols], ones], axis=1))
        numer.append(jnp.where(first, sums[:rows, :LANES], sums[rows:, :LANES]))
        denom.append(jnp.where(first, sums[:rows, LANES:], sums[rows:, LANES:]))
    return jnp.concatenate(numer, axis=1), jnp.concatenate(denom, axis=1)


def keys_values(blocks, lookup_ref, content_ref, keys_ref, values_ref):
    nodes = jnp.concatenate([block[...] for block in blocks], axis=0)
    keys_ref[...] = head_normed(dot(nodes, lookup_ref[...])).astype(BF16)
    values_ref[...] = dot(nodes, content_ref[...]).astype(BF16)


def lineup_kernel(count, *refs):
    row = 0
    for block in refs[:count]:
        refs[-1][row : row + block.shape[0], :] = block[...]
        row += block.shape[0]


def lineup(blocks, after=()):
    rows = sum(block.shape[0] for block in blocks)
    width = blocks[0].shape[1]
    return pl.pallas_call(
        functools.partial(lineup_kernel, len(blocks)),
        out_shape=jax.ShapeDtypeStruct((rows, width), BF16),
        in_specs=[VMEM] * len(blocks) + [ANY] * len(after),
        out_specs=VMEM,
        compiler_params=params(4),
        cost_estimate=cost(0, 0, 1 << 19),
        name="lineup",
    )(*blocks, *after)


def prep_kernel(*refs):
    count = (len(refs) - 1) // 2
    sources, targets, sems = refs[:count], refs[count:-1], refs[-1]
    copies = [
        pltpu.make_async_copy(source, target, sems.at[i])
        for i, (source, target) in enumerate(zip(sources, targets))
    ]
    for copy in copies:
        copy.start()
    for copy in copies:
        copy.wait()


def prep(*arrays):
    return pl.pallas_call(
        prep_kernel,
        out_shape=tuple(jax.ShapeDtypeStruct(a.shape, a.dtype) for a in arrays),
        in_specs=[ANY] * len(arrays),
        out_specs=(VMEM,) * len(arrays),
        scratch_shapes=[pltpu.SemaphoreType.DMA((len(arrays),))],
        compiler_params=params(4),
        cost_estimate=cost(0, 0, 4 << 20),
        name="prep",
    )(*arrays)


def near_kernel(softness_ref, *refs):
    askers, blocks, (asking_ref, lookup_ref, content_ref) = refs[:4], refs[4:-10], refs[-10:-7]
    queries_ref, numer_ref, denom_ref, keys_ref, values_ref, temper, sem = refs[-7:]
    copy = pltpu.make_async_copy(softness_ref, temper, sem)
    copy.start()
    keys_values((askers[2],) + blocks, lookup_ref, content_ref, keys_ref, values_ref)
    rows = jnp.concatenate([block[...] for block in askers], axis=0)
    projected = head_normed(dot(rows, asking_ref[...]))
    copy.wait()
    width = asking_ref.shape[1]
    head = lax.broadcasted_iota(jnp.int32, (1, width), 1) // SUBSPACE_WIDTH
    scale = jnp.zeros((1, width), F32)
    for h in range(NUM_SUBSPACES):
        scale = jnp.where(head == h, temper[h], scale)
    scale = scale * (math.log2(math.e) / math.sqrt(SUBSPACE_WIDTH))
    queries = (projected * scale).astype(BF16)
    queries_ref[...] = queries
    numer_ref[...], denom_ref[...] = attend(queries, keys_ref, values_ref)


def near(softness, askers, blocks, asking, lookup, content):
    length, width = askers[0].shape
    rows, count = len(askers) * length, (1 + len(blocks)) * length
    return pl.pallas_call(
        near_kernel,
        out_shape=(
            jax.ShapeDtypeStruct((rows, width), BF16),
            jax.ShapeDtypeStruct((rows, width), F32),
            jax.ShapeDtypeStruct((rows, width), F32),
        ),
        in_specs=[ANY] + [VMEM] * (7 + len(blocks)),
        out_specs=(VMEM,) * 3,
        scratch_shapes=[pltpu.VMEM((count, width), BF16)] * 2
        + [pltpu.SMEM(softness.shape, F32), pltpu.SemaphoreType.DMA],
        compiler_params=params(16),
        cost_estimate=cost(8 * rows * count * width, rows * count * NUM_SUBSPACES, 4 << 20),
        name="near",
    )(softness, *askers, *blocks, asking, lookup, content)


def pack(numer, denom):
    lane = lax.broadcasted_iota(jnp.int32, (denom.shape[0], LANES), 1)
    sums = denom[:, :LANES]
    for pair in range(1, PAIRS):
        held = (lane % SUBSPACE_WIDTH) // 16 == pair
        sums = jnp.where(held, denom[:, pair * LANES : (pair + 1) * LANES], sums)
    high = sums.astype(BF16).astype(F32)
    sums = jnp.where(lane % 16 < 8, high, sums - high)
    return jnp.concatenate([numer.astype(BF16), sums.astype(BF16)], axis=1)


def unpack_denom(packed, width):
    lane = lax.broadcasted_iota(jnp.int32, (LANES, width), 0)
    col = lax.broadcasted_iota(jnp.int32, (LANES, width), 1)
    half = (col % LANES) // SUBSPACE_WIDTH
    source = half * SUBSPACE_WIDTH + (col // LANES) * 16
    spread = jnp.where((lane == source) | (lane == source + 8), 1.0, 0.0).astype(BF16)
    return dot(packed, spread)


def call(kernel, steps, parts, wholes, out_parts, out_wholes, scratch, estimate, name, after=()):
    taken = len(parts) + len(wholes)

    def body(*refs):
        kernel(steps, *refs[:taken], *refs[taken + len(after) :])

    if steps == 1:
        grid, part, whole = (), lambda a: VMEM, lambda a: VMEM
    else:
        grid = (steps,)
        part = lambda a: pl.BlockSpec((a.shape[0] // steps,) + a.shape[1:], lambda i: (i, 0))
        whole = lambda a: pl.BlockSpec(a.shape, lambda i: (0, 0))
    return pl.pallas_call(
        body,
        grid=grid,
        out_shape=tuple(out_parts) + tuple(out_wholes),
        in_specs=[part(a) for a in parts] + [whole(a) for a in wholes] + [ANY] * len(after),
        out_specs=tuple(part(a) for a in out_parts) + tuple(whole(a) for a in out_wholes),
        scratch_shapes=scratch,
        compiler_params=params(16),
        cost_estimate=estimate,
        name=name,
    )(*parts, *wholes, *after)


def at_step(steps, step, body):
    if steps == 1:
        body()
    else:
        pl.when(pl.program_id(0) == step)(body)


def far_kernel(steps, *refs):
    blocks, (lookup_ref, content_ref, queries_ref, numer_ref, denom_ref) = refs[:-10], refs[-10:-5]
    keys_ref, values_ref, packed_ref, numer_sum, denom_sum = refs[-5:]
    half = queries_ref.shape[0] // 2

    def start():
        numer_sum[...] = numer_ref[:half, :]
        denom_sum[...] = denom_ref[:half, :]

    def end():
        packed_ref[...] = pack(numer_sum[...], denom_sum[...])

    at_step(steps, 0, start)
    keys_values(blocks, lookup_ref, content_ref, keys_ref, values_ref)
    numer, denom = attend(queries_ref[:half, :], keys_ref, values_ref)
    numer_sum[...] += numer
    denom_sum[...] += denom
    at_step(steps, steps - 1, end)


def far(blocks, block_len, lookup, content, queries, numer, denom, after):
    rows, width = queries.shape
    half = rows // 2
    count = len(blocks) * blocks[0].shape[0]
    kept = jax.ShapeDtypeStruct((count, width), BF16)
    return call(
        far_kernel,
        blocks[0].shape[0] // block_len,
        blocks,
        (lookup, content, queries, numer, denom),
        (kept, kept),
        (jax.ShapeDtypeStruct((half, width + LANES), BF16),),
        [pltpu.VMEM((half, width), F32)] * 2,
        cost(6 * half * count * width, half * count * NUM_SUBSPACES, 4 << 20),
        "far",
        after,
    )


def rest_kernel(steps, keys_ref, values_ref, queries_ref, numer_ref, denom_ref, numer_out, denom_out):
    half = queries_ref.shape[0] // 2

    def start():
        numer_out[...] = numer_ref[half:, :]
        denom_out[...] = denom_ref[half:, :]

    at_step(steps, 0, start)
    numer, denom = attend(queries_ref[half:, :], keys_ref, values_ref)
    numer_out[...] += numer
    denom_out[...] += denom


def rest(keys, values, steps, queries, numer, denom):
    rows, width = queries.shape
    half = rows // 2
    count = keys.shape[0]
    return call(
        rest_kernel,
        steps,
        (keys, values),
        (queries, numer, denom),
        (),
        (jax.ShapeDtypeStruct((half, width), F32),) * 2,
        [],
        cost(4 * half * count * width, half * count * NUM_SUBSPACES, 4 << 20),
        "rest",
    )


def combine_kernel(numer_ref, denom_ref, packed_ref, numer_out, denom_out, packed_out):
    rows, width = numer_out.shape
    numer = numer_ref[...] + packed_ref[:, :width].astype(F32)
    denom = denom_ref[...] + unpack_denom(packed_ref[:, width:], width)
    numer_out[...] = numer[:rows]
    denom_out[...] = denom[:rows]
    packed_out[...] = pack(numer[rows:], denom[rows:])


def combine(numer, denom, packed):
    rows, width = numer.shape[0] // 2, numer.shape[1]
    return pl.pallas_call(
        combine_kernel,
        out_shape=(
            jax.ShapeDtypeStruct((rows, width), F32),
            jax.ShapeDtypeStruct((rows, width), F32),
            jax.ShapeDtypeStruct((rows, width + LANES), BF16),
        ),
        in_specs=[VMEM] * 3,
        out_specs=(VMEM,) * 3,
        compiler_params=params(16),
        cost_estimate=cost(4 * rows * width * LANES, 0, 1 << 20),
        name="combine",
    )(numer, denom, packed)


def message_kernel(slots_ref, tiles_ref, *refs):
    blocks, (inner_ref, outer_ref, local_ref, slots, sem) = refs[:7], refs[7:]
    copy = pltpu.make_async_copy(slots_ref, slots, sem)
    copy.start()
    group = slots_ref.shape[0] // 3
    me, odd = lax.axis_index("head"), lax.axis_index("dom") % 2
    beside, beyond = 2 - 2 * odd, 2 * odd
    order = [(1, 0), (1, 1), (1, 2), (beside, 0), (beside, 2), (beyond, 0), (beyond, 2)]
    order += [(1, 3), (beside, 1), (beside, 3), (beyond, 1), (beyond, 3)]
    copy.wait()
    tiles = []
    for side, offset in order:
        tile_id = slots[side * group + (me ^ offset)]
        tile = tiles_ref[jnp.maximum(tile_id, 0)]
        tiles.append(jnp.where(tile_id >= 0, tile, jnp.zeros_like(tile)))
    nodes = jnp.concatenate([block[...] for block in blocks], axis=0)
    aggregate = dot(jnp.concatenate(tiles, axis=1), nodes).astype(BF16)
    hidden = jax.nn.gelu(dot(aggregate, inner_ref[...])).astype(BF16)
    local_ref[...] = dot(hidden, outer_ref[...])


def message(slots, tiles, blocks, inner, outer):
    rows, width = blocks[0].shape
    hidden = inner.shape[1]
    return pl.pallas_call(
        message_kernel,
        out_shape=jax.ShapeDtypeStruct((rows, width), F32),
        in_specs=[ANY] + [VMEM] * 10,
        out_specs=VMEM,
        scratch_shapes=[pltpu.SMEM(slots.shape, jnp.int32), pltpu.SemaphoreType.DMA],
        compiler_params=params(16),
        cost_estimate=cost(
            2 * rows * width * (12 * rows + 2 * hidden), rows * hidden, 4 << 20
        ),
        name="message",
    )(slots, tiles, *blocks, inner, outer)


def finish_kernel(
    numer_ref, denom_ref, packed_ref, final_ref, gain_ref, local_ref, nodes_ref, out_ref
):
    width = numer_ref.shape[1]
    numer = numer_ref[...] + packed_ref[:, :width].astype(F32)
    denom = denom_ref[...] + unpack_denom(packed_ref[:, width:], width)
    mixed = (numer / denom).astype(BF16)
    attended = dot(mixed, final_ref[...])
    mean = jnp.mean(attended * attended, axis=-1, keepdims=True)
    normed = attended * lax.rsqrt(mean + norm_eps) * gain_ref[...]
    out_ref[...] = (nodes_ref[...].astype(F32) + local_ref[...] + normed).astype(BF16)


def finish(numer, denom, packed, final, gain, local, nodes):
    rows, width = nodes.shape
    return pl.pallas_call(
        finish_kernel,
        out_shape=jax.ShapeDtypeStruct((rows, width), BF16),
        in_specs=[VMEM] * 7,
        out_specs=VMEM,
        compiler_params=params(16),
        cost_estimate=cost(2 * rows * width * width, rows, 2 << 20),
        name="finish",
    )(numer, denom, packed, final, gain, local, nodes)


def shards(
    vertex_embeddings,
    adjacent_group_bank_ids,
    coupling_strength_panels,
    asking_projector,
    lookup_projector,
    content_projector,
    final_projector,
    passing_inner_coefficients,
    passing_outer_coefficients,
    softness_per_subspace,
    mixing_layer_gain,
):
    block_len = vertex_embeddings.shape[0]
    doms = lax.axis_size("dom")
    nodes = vertex_embeddings
    stacked = lambda *arrays: jnp.concatenate(arrays, axis=0)

    distant = swap(nodes, "dom", 4)
    mask = 8
    while mask < doms:
        distant = stacked(distant, swap(stacked(nodes, distant), "dom", mask))
        mask *= 2

    def plane(block):
        side = swap(block, "dom", 1)
        below = swap(block, "head", 2)
        across = swap_both(block, 1, 2)
        return below, side, across

    near_blocks = plane(nodes)
    other = swap(nodes, "dom", 2)
    twin = swap(nodes, "head", 1)
    other_twin = swap_both(nodes, 2, 1)
    far_blocks = plane(distant)
    steps = distant.shape[0] // block_len
    if steps == 1:
        early = near_blocks + (distant,)
    else:
        early, far_blocks = near_blocks, (distant,) + far_blocks
    asking, lookup, content = prep(asking_projector, lookup_projector, content_projector)
    queries, numer, denom = near(
        softness_per_subspace, (twin, other_twin, nodes, other), early, asking, lookup, content
    )

    below, side, across = near_blocks
    pairs = [(p, p + 2) for p in range(0, doms - 2, 2)] + [(p, p - 2) for p in range(3, doms, 2)]
    halo = lax.ppermute(lineup((side, across), (distant, below)), "dom", pairs)
    keys, values, packed = far(
        far_blocks, block_len, lookup, content, queries, numer, denom, (halo,)
    )
    packed = swap(packed, "head", 1)
    numer, denom = rest(keys, values, steps, queries, numer, denom)
    numer, denom, packed = combine(numer, denom, packed)
    packed = swap(packed, "dom", 2)
    halo_twins = swap(lineup((below, side, across, halo), (numer,)), "head", 1)
    local = message(
        adjacent_group_bank_ids.reshape(-1),
        coupling_strength_panels,
        (nodes, twin, below, side, across, halo, halo_twins),
        passing_inner_coefficients,
        passing_outer_coefficients,
    )
    return finish(
        numer, denom, packed, final_projector, mixing_layer_gain.reshape(1, -1), local, nodes
    )


def solution(mesh):
    in_specs = (P(("dom", "head"), None), P("dom", "head", None)) + (P(),) * 9
    out_specs = P(("dom", "head"), None)
    return jax.shard_map(shards, mesh=mesh, in_specs=in_specs, out_specs=out_specs, check_vma=False)
```

```python
import functools
import math

import jax
import jax.numpy as jnp
from jax import lax
from jax.experimental import pallas as pl
from jax.experimental.pallas import tpu as pltpu
from jax.sharding import PartitionSpec as P

NUM_SUBSPACES = 8
SUBSPACE_WIDTH = 64
PAIRS = NUM_SUBSPACES // 2
PARTS = 2 * NUM_SUBSPACES
LANES = 128
norm_eps = 1e-06
VMEM = pl.BlockSpec(memory_space=pltpu.VMEM)
ANY = pl.BlockSpec(memory_space=pl.ANY)
F32 = jnp.float32
BF16 = jnp.bfloat16


def params(mebibytes):
    return pltpu.CompilerParams(vmem_limit_bytes=mebibytes << 20)


def cost(flops, transcendentals, data):
    return pl.CostEstimate(
        flops=flops // 16, transcendentals=transcendentals // 16, bytes_accessed=data // 16
    )


def swap(array, axis, mask):
    devices = lax.axis_size(axis)
    return lax.ppermute(array, axis, [(i, i ^ mask) for i in range(devices)])


def swap_both(array, dom_mask, head_mask):
    doms, heads = lax.axis_size("dom"), lax.axis_size("head")
    pairs = [
        (d * heads + h, (d ^ dom_mask) * heads + (h ^ head_mask))
        for d in range(doms)
        for h in range(heads)
    ]
    return lax.ppermute(array, ("dom", "head"), pairs)


def swap_by_core(array, first, second):
    doms, heads = lax.axis_size("dom"), lax.axis_size("head")
    pairs = []
    for d in range(doms):
        for h in range(heads):
            dom_mask, head_mask = second if h % 2 else first
            pairs.append((d * heads + h, (d ^ dom_mask) * heads + (h ^ head_mask)))
    return lax.ppermute(array, ("dom", "head"), pairs)


def dot(a, b):
    return jnp.dot(a, b, preferred_element_type=F32)


def dot_t(a, b):
    return lax.dot_general(a, b, (((1,), (1,)), ((), ())), preferred_element_type=F32)


def same_head(rows, cols, value):
    row = lax.broadcasted_iota(jnp.int32, (rows, cols), 0) // SUBSPACE_WIDTH
    col = lax.broadcasted_iota(jnp.int32, (rows, cols), 1) // SUBSPACE_WIDTH
    return jnp.where(row == col, value, 0.0).astype(BF16)


def head_normed(projected):
    block = same_head(256, 256, 1.0 / SUBSPACE_WIDTH)
    squares = (projected * projected).astype(BF16)
    mean = jnp.concatenate(
        [dot(squares[:, i : i + 256], block) for i in range(0, projected.shape[1], 256)], axis=1
    )
    return projected * lax.rsqrt(mean + norm_eps)


def padded_queries(queries, pair):
    both = queries[:, pair * LANES : (pair + 1) * LANES]
    first = lax.broadcasted_iota(jnp.int32, both.shape, 1) < SUBSPACE_WIDTH
    zero = jnp.zeros_like(both)
    return jnp.concatenate([jnp.where(first, both, zero), jnp.where(first, zero, both)], axis=0)


def attend(queries, keys_ref, values_ref):
    rows = queries.shape[0]
    count = keys_ref.shape[0]
    ones = jnp.ones((count, LANES), BF16)
    numer, denom = [], []
    first = lax.broadcasted_iota(jnp.int32, (rows, LANES), 1) < SUBSPACE_WIDTH
    for pair in range(PAIRS):
        cols = slice(pair * LANES, (pair + 1) * LANES)
        scores = dot_t(padded_queries(queries, pair), keys_ref[:, cols])
        weights = jnp.exp2(scores).astype(BF16)
        sums = dot(weights, jnp.concatenate([values_ref[:, cols], ones], axis=1))
        numer.append(jnp.where(first, sums[:rows, :LANES], sums[rows:, :LANES]))
        denom.append(jnp.where(first, sums[:rows, LANES:], sums[rows:, LANES:]))
    return jnp.concatenate(numer, axis=1), jnp.concatenate(denom, axis=1)


def keys_values(blocks, lookup_ref, content_ref, keys_ref, values_ref):
    nodes = jnp.concatenate(blocks, axis=0)
    keys_ref[...] = head_normed(dot(nodes, lookup_ref[...])).astype(BF16)
    values_ref[...] = dot(nodes, content_ref[...]).astype(BF16)


def lineup_kernel(count, rows, *refs):
    row = 0
    for block in refs[:count]:
        taken = min(block.shape[0], rows - row)
        refs[-1][row : row + taken, :] = block[:taken, :]
        row += taken


def lineup(blocks, after=(), rows=None, work=1 << 15):
    if rows is None:
        rows = sum(block.shape[0] for block in blocks)
    width = blocks[0].shape[1]
    return pl.pallas_call(
        functools.partial(lineup_kernel, len(blocks), rows),
        out_shape=jax.ShapeDtypeStruct((rows, width), BF16),
        in_specs=[VMEM] * len(blocks) + [ANY] * len(after),
        out_specs=VMEM,
        compiler_params=params(4),
        cost_estimate=pl.CostEstimate(flops=0, transcendentals=0, bytes_accessed=work),
        name="lineup",
    )(*blocks, *after)


def rows_kernel(start, block_ref, *refs):
    refs[-1][...] = block_ref[start : start + refs[-1].shape[0], :]


def rows_of(block, start, count, after=()):
    return pl.pallas_call(
        functools.partial(rows_kernel, start),
        out_shape=jax.ShapeDtypeStruct((count, block.shape[1]), BF16),
        in_specs=[VMEM] + [ANY] * len(after),
        out_specs=VMEM,
        compiler_params=params(4),
        cost_estimate=cost(0, 0, 1 << 19),
        name="rows",
    )(block, *after)


def near_kernel(softness_ref, both_ref, others_ref, *refs):
    blocks, (asking_ref, lookup_ref, content_ref) = refs[:-10], refs[-10:-7]
    queries_ref, keys_ref, values_ref, numer_ref, denom_ref, temper, sem = refs[-7:]
    half = both_ref.shape[0] // 2
    mine, theirs = slice(0, half), slice(half, 2 * half)
    copy = pltpu.make_async_copy(softness_ref, temper, sem)
    copy.start()
    nodes = [both_ref[mine, :]] + [block[...] for block in blocks]
    keys_values(nodes, lookup_ref, content_ref, keys_ref, values_ref)
    rows = jnp.concatenate(
        [others_ref[theirs, :], others_ref[mine, :], both_ref[theirs, :], both_ref[mine, :]], axis=0
    )
    projected = head_normed(dot(rows, asking_ref[...]))
    copy.wait()
    width = asking_ref.shape[1]
    head = lax.broadcasted_iota(jnp.int32, (1, width), 1) // SUBSPACE_WIDTH
    scale = jnp.zeros((1, width), F32)
    for h in range(NUM_SUBSPACES):
        scale = jnp.where(head == h, temper[h], scale)
    scale = scale * (math.log2(math.e) / math.sqrt(SUBSPACE_WIDTH))
    queries = (projected * scale).astype(BF16)
    queries_ref[...] = queries
    numer_ref[...], denom_ref[...] = attend(queries[: 2 * half], keys_ref, values_ref)


def near(softness, both, others, blocks, asking, lookup, content):
    rows, width = both.shape
    count = rows // 2 + sum(block.shape[0] for block in blocks)
    array = lambda n, dtype: jax.ShapeDtypeStruct((n, width), dtype)
    return pl.pallas_call(
        near_kernel,
        out_shape=(array(2 * rows, BF16),) + (array(count, BF16),) * 2 + (array(rows, F32),) * 2,
        in_specs=[ANY] + [VMEM] * (5 + len(blocks)),
        out_specs=(VMEM,) * 5,
        scratch_shapes=[pltpu.SMEM(softness.shape, F32), pltpu.SemaphoreType.DMA],
        compiler_params=params(16),
        cost_estimate=cost(6 * rows * count * width, rows * count * NUM_SUBSPACES, 4 << 20),
        name="near",
    )(softness, both, others, *blocks, asking, lookup, content)


def pack(numer, denom):
    lane = lax.broadcasted_iota(jnp.int32, (denom.shape[0], LANES), 1)
    sums = denom[:, :LANES]
    for pair in range(1, PAIRS):
        held = (lane % SUBSPACE_WIDTH) // 16 == pair
        sums = jnp.where(held, denom[:, pair * LANES : (pair + 1) * LANES], sums)
    high = sums.astype(BF16).astype(F32)
    sums = jnp.where(lane % 16 < 8, high, sums - high)
    return jnp.concatenate([numer.astype(BF16), sums.astype(BF16)], axis=1)


def unpack_denom(packed, width):
    lane = lax.broadcasted_iota(jnp.int32, (LANES, width), 0)
    col = lax.broadcasted_iota(jnp.int32, (LANES, width), 1)
    half = (col % LANES) // SUBSPACE_WIDTH
    source = half * SUBSPACE_WIDTH + (col // LANES) * 16
    spread = jnp.where((lane == source) | (lane == source + 8), 1.0, 0.0).astype(BF16)
    return dot(packed, spread)


def denom_rows(denom):
    row = lax.broadcasted_iota(jnp.int32, (PARTS, denom.shape[1]), 0)
    col = lax.broadcasted_iota(jnp.int32, (PARTS, denom.shape[1]), 1)
    high = denom.astype(BF16)
    low = (denom - high.astype(F32)).astype(BF16)
    first = jnp.where(col == row * SUBSPACE_WIDTH, 1.0, 0.0).astype(BF16)
    second = jnp.where(col == (row - NUM_SUBSPACES) * SUBSPACE_WIDTH, 1.0, 0.0).astype(BF16)
    return (dot_t(first, high) + dot_t(second, low)).astype(BF16)


def spread_denom(rows, width):
    row = lax.broadcasted_iota(jnp.int32, (PARTS, width), 0)
    head = lax.broadcasted_iota(jnp.int32, (PARTS, width), 1) // SUBSPACE_WIDTH
    spread = jnp.where(row % NUM_SUBSPACES == head, 1.0, 0.0).astype(BF16)
    return lax.dot_general(
        rows, spread, (((0,), (0,)), ((), ())), preferred_element_type=F32
    )


def call(kernel, steps, parts, wholes, out_parts, out_wholes, scratch, estimate, name, after=()):
    taken = len(parts) + len(wholes)

    def body(*refs):
        kernel(steps, *refs[:taken], *refs[taken + len(after) :])

    if steps == 1:
        grid, part, whole = (), lambda a: VMEM, lambda a: VMEM
    else:
        grid = (steps,)
        part = lambda a: pl.BlockSpec((a.shape[0] // steps,) + a.shape[1:], lambda i: (i, 0))
        whole = lambda a: pl.BlockSpec(a.shape, lambda i: (0, 0))
    return pl.pallas_call(
        body,
        grid=grid,
        out_shape=tuple(out_parts) + tuple(out_wholes),
        in_specs=[part(a) for a in parts] + [whole(a) for a in wholes] + [ANY] * len(after),
        out_specs=tuple(part(a) for a in out_parts) + tuple(whole(a) for a in out_wholes),
        scratch_shapes=scratch,
        compiler_params=params(16),
        cost_estimate=estimate,
        name=name,
    )(*parts, *wholes, *after)


def at_step(steps, step, body):
    if steps == 1:
        body()
    else:
        pl.when(pl.program_id(0) == step)(body)


def far_kernel(steps, *refs):
    blocks, (lookup_ref, content_ref, queries_ref, numer_ref, denom_ref) = refs[:-12], refs[-12:-7]
    keys_ref, values_ref, packed_ref, numer_out, denom_out, numer_sum, denom_sum = refs[-7:]
    pair = numer_ref.shape[0]
    half = pair // 2

    def start():
        numer_sum[...] = numer_ref[...]
        denom_sum[...] = denom_ref[...]

    def end():
        packed_ref[...] = pack(numer_sum[...], denom_sum[...])
        numer_out[...] = numer_sum[half:, :]
        denom_out[...] = denom_sum[half:, :]

    at_step(steps, 0, start)
    nodes = [block[...] for block in blocks]
    keys_values(nodes, lookup_ref, content_ref, keys_ref, values_ref)
    numer, denom = attend(queries_ref[:pair, :], keys_ref, values_ref)
    numer_sum[...] += numer
    denom_sum[...] += denom
    at_step(steps, steps - 1, end)


def far(blocks, block_len, lookup, content, queries, numer, denom):
    rows, width = numer.shape
    half = rows // 2
    count = len(blocks) * blocks[0].shape[0]
    kept = jax.ShapeDtypeStruct((count, width), BF16)
    return call(
        far_kernel,
        blocks[0].shape[0] // block_len,
        blocks,
        (lookup, content, queries, numer, denom),
        (kept, kept),
        (jax.ShapeDtypeStruct((rows, width + LANES), BF16),)
        + (jax.ShapeDtypeStruct((half, width), F32),) * 2,
        [pltpu.VMEM((rows, width), F32)] * 2,
        cost(6 * rows * count * width, rows * count * NUM_SUBSPACES, 4 << 20),
        "far",
    )


def own_kernel(steps, far_keys, far_values, queries_ref, near_keys, near_values, *refs):
    sent_ref, numer_out, denom_out, numer_sum, denom_sum = refs
    rows, width = numer_sum.shape
    half = rows // 2

    def start():
        numer_sum[...], denom_sum[...] = attend(queries_ref[rows:, :], near_keys, near_values)

    def end():
        sent_ref[:half, :] = numer_sum[:half, :].astype(BF16)
        sent_ref[half:, :] = jnp.zeros((PARTS, width), BF16)
        sent_ref[half:, :half] = denom_rows(denom_sum[:half, :])
        numer_out[...] = numer_sum[half:, :]
        denom_out[...] = denom_sum[half:, :]

    at_step(steps, 0, start)
    numer, denom = attend(queries_ref[rows:, :], far_keys, far_values)
    numer_sum[...] += numer
    denom_sum[...] += denom
    at_step(steps, steps - 1, end)


def own(far_keys, far_values, steps, queries, near_keys, near_values, after):
    rows, width = queries.shape[0] // 2, queries.shape[1]
    half = rows // 2
    return call(
        own_kernel,
        steps,
        (far_keys, far_values),
        (queries, near_keys, near_values),
        (),
        (jax.ShapeDtypeStruct((half + PARTS, width), BF16),)
        + (jax.ShapeDtypeStruct((half, width), F32),) * 2,
        [pltpu.VMEM((rows, width), F32)] * 2,
        cost(4 * rows * near_keys.shape[0] * width, 1 << 20, 4 << 20),
        "own",
        after,
    )


def combine_kernel(numer_ref, denom_ref, packed_ref, packed_out):
    rows, width = numer_ref.shape
    numer = numer_ref[...] + packed_ref[:rows, :width].astype(F32)
    denom = denom_ref[...] + unpack_denom(packed_ref[:rows, width:], width)
    packed_out[...] = pack(numer, denom)


def combine(numer, denom, packed):
    return pl.pallas_call(
        combine_kernel,
        out_shape=jax.ShapeDtypeStruct((numer.shape[0], packed.shape[1]), BF16),
        in_specs=[VMEM] * 3,
        out_specs=VMEM,
        compiler_params=params(8),
        cost_estimate=cost(4 * packed.shape[0] * packed.shape[1] * LANES, 0, 1 << 20),
        name="combine",
    )(numer, denom, packed)


def message_kernel(slots_ref, tiles_ref, *refs):
    both_ref, side_ref, across_ref, halo_ref, got_ref, *got_halo = refs[:8]
    inner_ref, outer_ref, gain_ref, local_ref, gain_out, slots, sem = refs[8:]
    gain_out[...] = gain_ref[...]
    copy = pltpu.make_async_copy(slots_ref, slots, sem)
    copy.start()
    group = slots_ref.shape[0] // 3
    me, core, odd = lax.axis_index("head"), lax.axis_index("head") % 2, lax.axis_index("dom") % 2
    beside, beyond = 2 - 2 * odd, 2 * odd
    part, parts = lax.axis_index("dom"), lax.axis_size("dom")
    outside = (part == 0) | (part == parts - 1)
    pick = lambda first, second: first + core * (second - first)
    order = [(1, 0), (1, 1)]
    order += [(pick(beside, 1), pick(0, 2)), (pick(beside, 1), pick(1, 3)), (beside, 2)]
    order += [(pick(1, beside), pick(3, 1)), (pick(1, beside), pick(2, 0)), (beside, 3)]
    order += [(beyond, core), (beyond, 1 - core), (beyond, 2), (beyond, 3)]
    rows = across_ref.shape[0]
    kept = halo_ref[: 2 * rows, :]
    sent = jnp.concatenate([got_halo[0][...], got_halo[1][...]], axis=0)
    nodes = [both_ref[...], side_ref[...], across_ref[...], got_ref[...]]
    nodes += [jnp.where(core == 0, kept, sent), halo_ref[2 * rows :, :], got_halo[2][...]]
    copy.wait()
    tiles = []
    for side, offset in order:
        tile_id = slots[side * group + (me ^ offset)]
        tile_id = jnp.where(outside & (side == beyond), -1, tile_id)
        tile = tiles_ref[jnp.maximum(tile_id, 0)]
        tiles.append(jnp.where(tile_id >= 0, tile, jnp.zeros_like(tile)))
    aggregate = dot(jnp.concatenate(tiles, axis=1), jnp.concatenate(nodes, axis=0)).astype(BF16)
    hidden = jax.nn.gelu(dot(aggregate, inner_ref[...])).astype(BF16)
    local_ref[...] = dot(hidden, outer_ref[...])


def message(slots, tiles, blocks, inner, outer, gain):
    rows, width, hidden = tiles.shape[1], inner.shape[0], inner.shape[1]
    return pl.pallas_call(
        message_kernel,
        out_shape=(jax.ShapeDtypeStruct((rows, width), F32), jax.ShapeDtypeStruct(gain.shape, F32)),
        in_specs=[ANY] + [VMEM] * (4 + len(blocks)),
        out_specs=(VMEM,) * 2,
        scratch_shapes=[pltpu.SMEM(slots.shape, jnp.int32), pltpu.SemaphoreType.DMA],
        compiler_params=params(16),
        cost_estimate=cost(
            2 * rows * width * (12 * rows + 2 * hidden), rows * hidden, 4 << 20
        ),
        name="message",
    )(slots, tiles, *blocks, inner, outer, gain)


def finish_kernel(
    numer_ref, denom_ref, crossed_ref, packed_ref, final_ref, gain_ref, local_ref, nodes_ref, out_ref
):
    width = numer_ref.shape[1]
    rows = numer_ref.shape[0]
    numer = numer_ref[...] + crossed_ref[:rows, :].astype(F32) + packed_ref[:, :width].astype(F32)
    denom = denom_ref[...] + spread_denom(crossed_ref[rows:, :rows], width)
    denom += unpack_denom(packed_ref[:, width:], width)
    mixed = (numer / denom).astype(BF16)
    attended = dot(mixed, final_ref[...])
    mean = jnp.mean(attended * attended, axis=-1, keepdims=True)
    normed = attended * lax.rsqrt(mean + norm_eps) * gain_ref[...]
    out_ref[...] = (nodes_ref[...].astype(F32) + local_ref[...] + normed).astype(BF16)


def finish(numer, denom, crossed, packed, final, gain, local, nodes):
    rows, width = nodes.shape
    return pl.pallas_call(
        finish_kernel,
        out_shape=jax.ShapeDtypeStruct((rows, width), BF16),
        in_specs=[VMEM] * 8,
        out_specs=VMEM,
        compiler_params=params(16),
        cost_estimate=cost(2 * rows * width * width, rows, 2 << 20),
        name="finish",
    )(numer, denom, crossed, packed, final, gain, local, nodes)


def shards(
    vertex_embeddings,
    adjacent_group_bank_ids,
    coupling_strength_panels,
    asking_projector,
    lookup_projector,
    content_projector,
    final_projector,
    passing_inner_coefficients,
    passing_outer_coefficients,
    softness_per_subspace,
    mixing_layer_gain,
):
    block_len = vertex_embeddings.shape[0]
    doms = lax.axis_size("dom")
    nodes = vertex_embeddings
    stacked = lambda *arrays: jnp.concatenate(arrays, axis=0)

    distant = swap(nodes, "dom", 4)
    mask = 8
    while mask < doms:
        distant = stacked(distant, swap(stacked(nodes, distant), "dom", mask))
        mask *= 2

    def plane(block):
        side = swap(block, "dom", 1)
        below = swap(block, "head", 2)
        across = swap_both(block, 1, 2)
        return below, side, across

    held = lineup((nodes,))
    if distant.shape[0] == block_len:
        distant = lineup((distant,), work=20 << 20)
    both = lineup((held, swap(nodes, "head", 1)))
    side = swap_by_core(both, (1, 0), (0, 2))
    across = swap_by_core(lineup((side,), (), block_len), (0, 2), (1, 0))
    other = swap(nodes, "dom", 2)
    others = lineup((other, swap(other, "head", 1)))
    far_blocks = plane(distant)
    steps = distant.shape[0] // block_len
    if steps == 1:
        early = (side, across, distant)
    else:
        early, far_blocks = (side, across), (distant,) + far_blocks
    queries, keys, values, numer, denom = near(
        softness_per_subspace,
        both,
        others,
        early,
        asking_projector,
        lookup_projector,
        content_projector,
    )

    pairs = [(p, p + 2) for p in range(0, doms - 2, 2)] + [(p, p - 2) for p in range(3, doms, 2)]
    halo = lax.ppermute(lineup((side, across), ()), "dom", pairs)
    far_keys, far_values, packed, numer, denom = far(
        far_blocks, block_len, lookup_projector, content_projector, queries, numer, denom
    )
    packed = packed_here = combine(numer, denom, swap(packed, "head", 1))
    crossed, numer, denom = own(far_keys, far_values, steps, queries, keys, values, (packed,))
    crossed = swap(crossed, "head", 1)
    packed = swap(packed, "dom", 2)
    got = swap(lineup((side, across)), "head", 1)
    got_halo = [
        swap(rows_of(halo, at * block_len, block_len, (numer,)), "head", 1) for at in range(3)
    ]
    local, gain = message(
        adjacent_group_bank_ids.reshape(-1),
        coupling_strength_panels,
        (both, side, across, halo, got, *got_halo),
        passing_inner_coefficients,
        passing_outer_coefficients,
        mixing_layer_gain.reshape(1, -1),
    )
    return finish(
        numer, denom, crossed, packed, final_projector, gain, local, held
    )


def solution(mesh):
    in_specs = (P(("dom", "head"), None), P("dom", "head", None)) + (P(),) * 9
    out_specs = P(("dom", "head"), None)
    return jax.shard_map(shards, mesh=mesh, in_specs=in_specs, out_specs=out_specs, check_vma=False)
```

```python
import functools
import math

import jax
import jax.numpy as jnp
from jax import lax
from jax.experimental import pallas as pl
from jax.experimental.pallas import tpu as pltpu
from jax.sharding import PartitionSpec as P

NUM_SUBSPACES = 8
SUBSPACE_WIDTH = 64
PAIRS = NUM_SUBSPACES // 2
PARTS = 2 * NUM_SUBSPACES
LANES = 128
norm_eps = 1e-06
VMEM = pl.BlockSpec(memory_space=pltpu.VMEM)
ANY = pl.BlockSpec(memory_space=pl.ANY)
F32 = jnp.float32
BF16 = jnp.bfloat16


def params(mebibytes):
    return pltpu.CompilerParams(vmem_limit_bytes=mebibytes << 20)


def cost(flops, transcendentals, data):
    return pl.CostEstimate(
        flops=flops // 16, transcendentals=transcendentals // 16, bytes_accessed=data // 16
    )


def swap(array, axis, mask):
    devices = lax.axis_size(axis)
    return lax.ppermute(array, axis, [(i, i ^ mask) for i in range(devices)])


def swap_both(array, dom_mask, head_mask):
    doms, heads = lax.axis_size("dom"), lax.axis_size("head")
    pairs = [
        (d * heads + h, (d ^ dom_mask) * heads + (h ^ head_mask))
        for d in range(doms)
        for h in range(heads)
    ]
    return lax.ppermute(array, ("dom", "head"), pairs)


def swap_by_core(array, first, second):
    doms, heads = lax.axis_size("dom"), lax.axis_size("head")
    pairs = []
    for d in range(doms):
        for h in range(heads):
            dom_mask, head_mask = second if h % 2 else first
            pairs.append((d * heads + h, (d ^ dom_mask) * heads + (h ^ head_mask)))
    return lax.ppermute(array, ("dom", "head"), pairs)


def dot(a, b):
    return jnp.dot(a, b, preferred_element_type=F32)


def dot_t(a, b):
    return lax.dot_general(a, b, (((1,), (1,)), ((), ())), preferred_element_type=F32)


def same_head(rows, cols, value):
    row = lax.broadcasted_iota(jnp.int32, (rows, cols), 0) // SUBSPACE_WIDTH
    col = lax.broadcasted_iota(jnp.int32, (rows, cols), 1) // SUBSPACE_WIDTH
    return jnp.where(row == col, value, 0.0).astype(BF16)


def head_normed(projected):
    block = same_head(256, 256, 1.0 / SUBSPACE_WIDTH)
    squares = (projected * projected).astype(BF16)
    mean = jnp.concatenate(
        [dot(squares[:, i : i + 256], block) for i in range(0, projected.shape[1], 256)], axis=1
    )
    return projected * lax.rsqrt(mean + norm_eps)


def padded_queries(queries, pair):
    both = queries[:, pair * LANES : (pair + 1) * LANES]
    first = lax.broadcasted_iota(jnp.int32, both.shape, 1) < SUBSPACE_WIDTH
    zero = jnp.zeros_like(both)
    return jnp.concatenate([jnp.where(first, both, zero), jnp.where(first, zero, both)], axis=0)


def attend(queries, keys_ref, values_ref):
    rows = queries.shape[0]
    count = keys_ref.shape[0]
    ones = jnp.ones((count, LANES), BF16)
    numer, denom = [], []
    first = lax.broadcasted_iota(jnp.int32, (rows, LANES), 1) < SUBSPACE_WIDTH
    for pair in range(PAIRS):
        cols = slice(pair * LANES, (pair + 1) * LANES)
        scores = dot_t(padded_queries(queries, pair), keys_ref[:, cols])
        weights = jnp.exp2(scores).astype(BF16)
        sums = dot(weights, jnp.concatenate([values_ref[:, cols], ones], axis=1))
        numer.append(jnp.where(first, sums[:rows, :LANES], sums[rows:, :LANES]))
        denom.append(jnp.where(first, sums[:rows, LANES:], sums[rows:, LANES:]))
    return jnp.concatenate(numer, axis=1), jnp.concatenate(denom, axis=1)


def keys_values(blocks, lookup_ref, content_ref, keys_ref, values_ref):
    nodes = jnp.concatenate(blocks, axis=0)
    keys_ref[...] = head_normed(dot(nodes, lookup_ref[...])).astype(BF16)
    values_ref[...] = dot(nodes, content_ref[...]).astype(BF16)


def lineup_kernel(count, rows, *refs):
    row = 0
    for block in refs[:count]:
        taken = min(block.shape[0], rows - row)
        refs[-1][row : row + taken, :] = block[:taken, :]
        row += taken


def lineup(blocks, after=(), rows=None, work=1 << 15):
    if rows is None:
        rows = sum(block.shape[0] for block in blocks)
    width = blocks[0].shape[1]
    return pl.pallas_call(
        functools.partial(lineup_kernel, len(blocks), rows),
        out_shape=jax.ShapeDtypeStruct((rows, width), BF16),
        in_specs=[VMEM] * len(blocks) + [ANY] * len(after),
        out_specs=VMEM,
        compiler_params=params(4),
        cost_estimate=pl.CostEstimate(flops=0, transcendentals=0, bytes_accessed=work),
        name="lineup",
    )(*blocks, *after)


def rows_kernel(start, block_ref, *refs):
    refs[-1][...] = block_ref[start : start + refs[-1].shape[0], :]


def rows_of(block, start, count, after=()):
    return pl.pallas_call(
        functools.partial(rows_kernel, start),
        out_shape=jax.ShapeDtypeStruct((count, block.shape[1]), BF16),
        in_specs=[VMEM] + [ANY] * len(after),
        out_specs=VMEM,
        compiler_params=params(4),
        cost_estimate=cost(0, 0, 1 << 19),
        name="rows",
    )(block, *after)


def early_kernel(softness_ref, slots_ref, both_ref, side_ref, asking_ref, lookup_ref, content_ref, *refs):
    queries_ref, scale_ref, keys_ref, values_ref, slots_out, temper, sems = refs
    half = both_ref.shape[0] // 2
    copies = [
        pltpu.make_async_copy(softness_ref, temper, sems.at[0]),
        pltpu.make_async_copy(slots_ref, slots_out, sems.at[1]),
    ]
    for copy in copies:
        copy.start()
    nodes = [both_ref[:half, :], side_ref[...]]
    keys_values(nodes, lookup_ref, content_ref, keys_ref, values_ref)
    projected = head_normed(dot(both_ref[...], asking_ref[...]))
    for copy in copies:
        copy.wait()
    width = asking_ref.shape[1]
    head = lax.broadcasted_iota(jnp.int32, (1, width), 1) // SUBSPACE_WIDTH
    scale = jnp.zeros((1, width), F32)
    for h in range(NUM_SUBSPACES):
        scale = jnp.where(head == h, temper[h], scale)
    scale = scale * (math.log2(math.e) / math.sqrt(SUBSPACE_WIDTH))
    scale_ref[...] = scale
    queries = (projected * scale).astype(BF16)
    queries_ref[:half, :] = queries[half:]
    queries_ref[half:, :] = queries[:half]


def early(softness, slots, both, side, asking, lookup, content):
    rows, width = both.shape
    count = rows // 2 + side.shape[0]
    array = lambda n, dtype: jax.ShapeDtypeStruct((n, width), dtype)
    return pl.pallas_call(
        early_kernel,
        out_shape=(array(rows, BF16), array(1, F32), array(count, BF16), array(count, BF16))
        + (jax.ShapeDtypeStruct(slots.shape, jnp.int32),),
        in_specs=[ANY] * 2 + [VMEM] * 5,
        out_specs=(VMEM,) * 5,
        scratch_shapes=[pltpu.SMEM(softness.shape, F32), pltpu.SemaphoreType.DMA((2,))],
        compiler_params=params(16),
        cost_estimate=cost(2 * (rows + 2 * count) * width * width, rows, 4 << 20),
        name="early",
    )(softness, slots, both, side, asking, lookup, content)


def near_kernel(scale_ref, held_keys, held_values, others_ref, *refs):
    blocks, (asking_ref, lookup_ref, content_ref) = refs[:-8], refs[-8:-5]
    queries_ref, keys_ref, values_ref, numer_ref, denom_ref = refs[-5:]
    half, held = others_ref.shape[0] // 2, held_keys.shape[0]
    keys_ref[:held, :] = held_keys[...]
    values_ref[:held, :] = held_values[...]
    nodes = [block[...] for block in blocks]
    keys_values(nodes, lookup_ref, content_ref, keys_ref.at[held:], values_ref.at[held:])
    rows = jnp.concatenate([others_ref[half:, :], others_ref[:half, :]], axis=0)
    queries = (head_normed(dot(rows, asking_ref[...])) * scale_ref[...]).astype(BF16)
    queries_ref[...] = queries
    numer_ref[...], denom_ref[...] = attend(queries, keys_ref, values_ref)


def near(scale, keys, values, others, blocks, asking, lookup, content):
    rows, width = others.shape
    count = keys.shape[0] + sum(block.shape[0] for block in blocks)
    array = lambda n, dtype: jax.ShapeDtypeStruct((n, width), dtype)
    return pl.pallas_call(
        near_kernel,
        out_shape=(array(rows, BF16),) + (array(count, BF16),) * 2 + (array(rows, F32),) * 2,
        in_specs=[VMEM] * (7 + len(blocks)),
        out_specs=(VMEM,) * 5,
        compiler_params=params(16),
        cost_estimate=cost(6 * rows * count * width, rows * count * NUM_SUBSPACES, 4 << 20),
        name="near",
    )(scale, keys, values, others, *blocks, asking, lookup, content)


def pack(numer, denom):
    lane = lax.broadcasted_iota(jnp.int32, (denom.shape[0], LANES), 1)
    sums = denom[:, :LANES]
    for pair in range(1, PAIRS):
        held = (lane % SUBSPACE_WIDTH) // 16 == pair
        sums = jnp.where(held, denom[:, pair * LANES : (pair + 1) * LANES], sums)
    high = sums.astype(BF16).astype(F32)
    sums = jnp.where(lane % 16 < 8, high, sums - high)
    return jnp.concatenate([numer.astype(BF16), sums.astype(BF16)], axis=1)


def unpack_denom(packed, width):
    lane = lax.broadcasted_iota(jnp.int32, (LANES, width), 0)
    col = lax.broadcasted_iota(jnp.int32, (LANES, width), 1)
    half = (col % LANES) // SUBSPACE_WIDTH
    source = half * SUBSPACE_WIDTH + (col // LANES) * 16
    spread = jnp.where((lane == source) | (lane == source + 8), 1.0, 0.0).astype(BF16)
    return dot(packed, spread)


def denom_rows(denom):
    row = lax.broadcasted_iota(jnp.int32, (PARTS, denom.shape[1]), 0)
    col = lax.broadcasted_iota(jnp.int32, (PARTS, denom.shape[1]), 1)
    high = denom.astype(BF16)
    low = (denom - high.astype(F32)).astype(BF16)
    first = jnp.where(col == row * SUBSPACE_WIDTH, 1.0, 0.0).astype(BF16)
    second = jnp.where(col == (row - NUM_SUBSPACES) * SUBSPACE_WIDTH, 1.0, 0.0).astype(BF16)
    return (dot_t(first, high) + dot_t(second, low)).astype(BF16)


def spread_denom(rows, width):
    row = lax.broadcasted_iota(jnp.int32, (PARTS, width), 0)
    head = lax.broadcasted_iota(jnp.int32, (PARTS, width), 1) // SUBSPACE_WIDTH
    spread = jnp.where(row % NUM_SUBSPACES == head, 1.0, 0.0).astype(BF16)
    return lax.dot_general(
        rows, spread, (((0,), (0,)), ((), ())), preferred_element_type=F32
    )


def call(kernel, steps, parts, wholes, out_parts, out_wholes, scratch, estimate, name, after=()):
    taken = len(parts) + len(wholes)

    def body(*refs):
        kernel(steps, *refs[:taken], *refs[taken + len(after) :])

    if steps == 1:
        grid, part, whole = (), lambda a: VMEM, lambda a: VMEM
    else:
        grid = (steps,)
        part = lambda a: pl.BlockSpec((a.shape[0] // steps,) + a.shape[1:], lambda i: (i, 0))
        whole = lambda a: pl.BlockSpec(a.shape, lambda i: (0, 0))
    return pl.pallas_call(
        body,
        grid=grid,
        out_shape=tuple(out_parts) + tuple(out_wholes),
        in_specs=[part(a) for a in parts] + [whole(a) for a in wholes] + [ANY] * len(after),
        out_specs=tuple(part(a) for a in out_parts) + tuple(whole(a) for a in out_wholes),
        scratch_shapes=scratch,
        compiler_params=params(16),
        cost_estimate=estimate,
        name=name,
    )(*parts, *wholes, *after)


def at_step(steps, step, body):
    if steps == 1:
        body()
    else:
        pl.when(pl.program_id(0) == step)(body)


def far_kernel(steps, *refs):
    blocks, (lookup_ref, content_ref, queries_ref, numer_ref, denom_ref) = refs[:-12], refs[-12:-7]
    keys_ref, values_ref, packed_ref, numer_out, denom_out, numer_sum, denom_sum = refs[-7:]
    pair = numer_ref.shape[0]
    half = pair // 2

    def start():
        numer_sum[...] = numer_ref[...]
        denom_sum[...] = denom_ref[...]

    def end():
        packed_ref[...] = pack(numer_sum[...], denom_sum[...])
        numer_out[...] = numer_sum[half:, :]
        denom_out[...] = denom_sum[half:, :]

    at_step(steps, 0, start)
    nodes = [block[...] for block in blocks]
    keys_values(nodes, lookup_ref, content_ref, keys_ref, values_ref)
    numer, denom = attend(queries_ref[:pair, :], keys_ref, values_ref)
    numer_sum[...] += numer
    denom_sum[...] += denom
    at_step(steps, steps - 1, end)


def far(blocks, block_len, lookup, content, queries, numer, denom):
    rows, width = numer.shape
    half = rows // 2
    count = len(blocks) * blocks[0].shape[0]
    kept = jax.ShapeDtypeStruct((count, width), BF16)
    return call(
        far_kernel,
        blocks[0].shape[0] // block_len,
        blocks,
        (lookup, content, queries, numer, denom),
        (kept, kept),
        (jax.ShapeDtypeStruct((rows, width + LANES), BF16),)
        + (jax.ShapeDtypeStruct((half, width), F32),) * 2,
        [pltpu.VMEM((rows, width), F32)] * 2,
        cost(6 * rows * count * width, rows * count * NUM_SUBSPACES, 4 << 20),
        "far",
    )


def own_first_kernel(queries_ref, keys_ref, values_ref, *refs):
    numer_ref, denom_ref = refs[-2:]
    count = 2 * queries_ref.shape[0]
    numer_ref[...], denom_ref[...] = attend(
        queries_ref[...], keys_ref.at[:count], values_ref.at[:count]
    )


def own_first(queries, keys, values, after):
    rows, width = queries.shape
    return pl.pallas_call(
        own_first_kernel,
        out_shape=(jax.ShapeDtypeStruct((rows, width), F32),) * 2,
        in_specs=[VMEM] * 3 + [ANY] * len(after),
        out_specs=(VMEM,) * 2,
        compiler_params=params(16),
        cost_estimate=cost(8 * rows * rows * width, 2 * rows * rows * NUM_SUBSPACES, 2 << 20),
        name="own_first",
    )(queries, keys, values, *after)


def own_kernel(steps, far_keys, far_values, queries_ref, near_keys, near_values, *refs):
    numer_ref, denom_ref, sent_ref, numer_out, denom_out = refs[:5]
    numer_sum, denom_sum, keys_ref, values_ref = refs[5:]
    rows, width = numer_sum.shape
    half, done, left = rows // 2, 2 * rows, near_keys.shape[0] - 2 * rows

    def start():
        numer_sum[...] = numer_ref[...]
        denom_sum[...] = denom_ref[...]

    def end():
        sent_ref[:half, :] = numer_sum[:half, :].astype(BF16)
        sent_ref[half:, :] = jnp.zeros((PARTS, width), BF16)
        sent_ref[half:, :half] = denom_rows(denom_sum[:half, :])
        numer_out[...] = numer_sum[half:, :]
        denom_out[...] = denom_sum[half:, :]

    at_step(steps, 0, start)
    if left:
        keys_ref[:left, :] = near_keys[done:, :]
        values_ref[:left, :] = near_values[done:, :]
        keys_ref[left:, :] = far_keys[...]
        values_ref[left:, :] = far_values[...]
        numer, denom = attend(queries_ref[...], keys_ref, values_ref)
    else:
        numer, denom = attend(queries_ref[...], far_keys, far_values)
    numer_sum[...] += numer
    denom_sum[...] += denom
    at_step(steps, steps - 1, end)


def own(far_keys, far_values, steps, queries, near_keys, near_values, numer, denom, after):
    rows, width = queries.shape
    half = rows // 2
    count = near_keys.shape[0] - 2 * rows + far_keys.shape[0] // steps
    return call(
        own_kernel,
        steps,
        (far_keys, far_values),
        (queries, near_keys, near_values, numer, denom),
        (),
        (jax.ShapeDtypeStruct((half + PARTS, width), BF16),)
        + (jax.ShapeDtypeStruct((half, width), F32),) * 2,
        [pltpu.VMEM((rows, width), F32)] * 2 + [pltpu.VMEM((count, width), BF16)] * 2,
        cost(4 * rows * count * width, rows * count * NUM_SUBSPACES, 4 << 20),
        "own",
        after,
    )


def combine_kernel(numer_ref, denom_ref, packed_ref, after_ref, packed_out):
    rows, width = numer_ref.shape
    numer = numer_ref[...] + packed_ref[:rows, :width].astype(F32)
    denom = denom_ref[...] + unpack_denom(packed_ref[:rows, width:], width)
    packed_out[...] = pack(numer, denom)


def combine(numer, denom, packed, after):
    return pl.pallas_call(
        combine_kernel,
        out_shape=jax.ShapeDtypeStruct((numer.shape[0], packed.shape[1]), BF16),
        in_specs=[VMEM] * 3 + [ANY],
        out_specs=VMEM,
        compiler_params=params(8),
        cost_estimate=cost(4 * packed.shape[0] * packed.shape[1] * LANES, 0, 1 << 20),
        name="combine",
    )(numer, denom, packed, *after)


def message_kernel(slots_ref, tiles_ref, *refs):
    both_ref, side_ref, across_ref, halo_ref, got_ref, *got_halo = refs[:8]
    inner_ref, outer_ref, gain_ref, local_ref, gain_out, slots, sem = refs[8:]
    gain_out[...] = gain_ref[...]
    copy = pltpu.make_async_copy(slots_ref, slots, sem)
    copy.start()
    group = slots_ref.shape[1] // 3
    me, core, odd = lax.axis_index("head"), lax.axis_index("head") % 2, lax.axis_index("dom") % 2
    beside, beyond = 2 - 2 * odd, 2 * odd
    part, parts = lax.axis_index("dom"), lax.axis_size("dom")
    outside = (part == 0) | (part == parts - 1)
    pick = lambda first, second: first + core * (second - first)
    order = [(1, 0), (1, 1)]
    order += [(pick(beside, 1), pick(0, 2)), (pick(beside, 1), pick(1, 3)), (beside, 2)]
    order += [(pick(1, beside), pick(3, 1)), (pick(1, beside), pick(2, 0)), (beside, 3)]
    order += [(beyond, core), (beyond, 1 - core), (beyond, 2), (beyond, 3)]
    rows = across_ref.shape[0]
    kept = halo_ref[: 2 * rows, :]
    sent = jnp.concatenate([got_halo[0][...], got_halo[1][...]], axis=0)
    nodes = [both_ref[...], side_ref[...], across_ref[...], got_ref[...]]
    nodes += [jnp.where(core == 0, kept, sent), halo_ref[2 * rows :, :], got_halo[2][...]]
    copy.wait()
    tiles = []
    for side, offset in order:
        tile_id = slots[0, side * group + (me ^ offset)]
        tile_id = jnp.where(outside & (side == beyond), -1, tile_id)
        tile = tiles_ref[jnp.maximum(tile_id, 0)]
        tiles.append(jnp.where(tile_id >= 0, tile, jnp.zeros_like(tile)))
    aggregate = dot(jnp.concatenate(tiles, axis=1), jnp.concatenate(nodes, axis=0)).astype(BF16)
    hidden = jax.nn.gelu(dot(aggregate, inner_ref[...])).astype(BF16)
    local_ref[...] = dot(hidden, outer_ref[...])


def message(slots, tiles, blocks, inner, outer, gain):
    rows, width, hidden = tiles.shape[1], inner.shape[0], inner.shape[1]
    return pl.pallas_call(
        message_kernel,
        out_shape=(jax.ShapeDtypeStruct((rows, width), F32), jax.ShapeDtypeStruct(gain.shape, F32)),
        in_specs=[VMEM] + [VMEM] * (4 + len(blocks)),
        out_specs=(VMEM,) * 2,
        scratch_shapes=[pltpu.SMEM(slots.shape, jnp.int32), pltpu.SemaphoreType.DMA],
        compiler_params=params(16),
        cost_estimate=cost(
            2 * rows * width * (12 * rows + 2 * hidden), rows * hidden, 4 << 20
        ),
        name="message",
    )(slots, tiles, *blocks, inner, outer, gain)


def finish_kernel(
    numer_ref, denom_ref, crossed_ref, packed_ref, final_ref, gain_ref, local_ref, nodes_ref, out_ref
):
    width = numer_ref.shape[1]
    rows = numer_ref.shape[0]
    numer = numer_ref[...] + crossed_ref[:rows, :].astype(F32) + packed_ref[:, :width].astype(F32)
    denom = denom_ref[...] + spread_denom(crossed_ref[rows:, :rows], width)
    denom += unpack_denom(packed_ref[:, width:], width)
    mixed = (numer / denom).astype(BF16)
    attended = dot(mixed, final_ref[...])
    mean = jnp.mean(attended * attended, axis=-1, keepdims=True)
    normed = attended * lax.rsqrt(mean + norm_eps) * gain_ref[...]
    out_ref[...] = (nodes_ref[...].astype(F32) + local_ref[...] + normed).astype(BF16)


def finish(numer, denom, crossed, packed, final, gain, local, nodes):
    rows, width = nodes.shape
    return pl.pallas_call(
        finish_kernel,
        out_shape=jax.ShapeDtypeStruct((rows, width), BF16),
        in_specs=[VMEM] * 8,
        out_specs=VMEM,
        compiler_params=params(16),
        cost_estimate=cost(2 * rows * width * width, rows, 2 << 20),
        name="finish",
    )(numer, denom, crossed, packed, final, gain, local, nodes)


def shards(
    vertex_embeddings,
    adjacent_group_bank_ids,
    coupling_strength_panels,
    asking_projector,
    lookup_projector,
    content_projector,
    final_projector,
    passing_inner_coefficients,
    passing_outer_coefficients,
    softness_per_subspace,
    mixing_layer_gain,
):
    block_len = vertex_embeddings.shape[0]
    doms = lax.axis_size("dom")
    nodes = vertex_embeddings
    stacked = lambda *arrays: jnp.concatenate(arrays, axis=0)

    distant = swap(nodes, "dom", 4)
    mask = 8
    while mask < doms:
        distant = stacked(distant, swap(stacked(nodes, distant), "dom", mask))
        mask *= 2

    def plane(block):
        side = swap(block, "dom", 1)
        below = swap(block, "head", 2)
        across = swap_both(block, 1, 2)
        return below, side, across

    held = lineup((nodes,))
    both = lineup((held, swap(nodes, "head", 1)))
    side = swap_by_core(both, (1, 0), (0, 2))
    across = swap_by_core(lineup((side,), (), block_len), (0, 2), (1, 0))
    other = swap(nodes, "dom", 2)
    others = lineup((other, swap(other, "head", 1)))
    queries, scale, keys, values, slots = early(
        softness_per_subspace,
        adjacent_group_bank_ids.reshape(1, -1),
        both,
        side,
        asking_projector,
        lookup_projector,
        content_projector,
    )
    distant = lineup((distant,), (queries,))
    far_blocks = plane(distant)
    steps = distant.shape[0] // block_len
    if steps == 1:
        near_blocks = (across, distant, far_blocks[1])
        far_blocks = (far_blocks[0], far_blocks[2])
    else:
        near_blocks, far_blocks = (across,), (distant,) + far_blocks
    pair_queries, keys, values, numer, denom = near(
        scale,
        keys,
        values,
        others,
        near_blocks,
        asking_projector,
        lookup_projector,
        content_projector,
    )

    pairs = [(p, p + 2) for p in range(0, doms - 2, 2)] + [(p, p - 2) for p in range(3, doms, 2)]
    halo = lax.ppermute(lineup((side, across), ()), "dom", pairs)
    far_keys, far_values, packed, numer, denom = far(
        far_blocks, block_len, lookup_projector, content_projector, pair_queries, numer, denom
    )
    own_numer, own_denom = own_first(queries, keys, values, (packed,))
    packed = combine(numer, denom, swap(packed, "head", 1), (own_numer,))
    crossed, numer, denom = own(
        far_keys, far_values, steps, queries, keys, values, own_numer, own_denom, (packed,)
    )
    crossed = swap(crossed, "head", 1)
    packed = swap(packed, "dom", 2)
    got = swap(lineup((side, across)), "head", 1)
    got_halo = [
        swap(rows_of(halo, at * block_len, block_len, (numer,)), "head", 1) for at in range(3)
    ]
    local, gain = message(
        slots,
        coupling_strength_panels,
        (both, side, across, halo, got, *got_halo),
        passing_inner_coefficients,
        passing_outer_coefficients,
        mixing_layer_gain.reshape(1, -1),
    )
    return finish(
        numer, denom, crossed, packed, final_projector, gain, local, held
    )


def solution(mesh):
    in_specs = (P(("dom", "head"), None), P("dom", "head", None)) + (P(),) * 9
    out_specs = P(("dom", "head"), None)
    return jax.shard_map(shards, mesh=mesh, in_specs=in_specs, out_specs=out_specs, check_vma=False)
```

```python
import functools
import math

import jax
import jax.numpy as jnp
from jax import lax
from jax.experimental import pallas as pl
from jax.experimental.pallas import tpu as pltpu
from jax.sharding import PartitionSpec as P

NUM_SUBSPACES = 8
SUBSPACE_WIDTH = 64
PAIRS = NUM_SUBSPACES // 2
PARTS = 2 * NUM_SUBSPACES
LANES = 128
norm_eps = 1e-06
VMEM = pl.BlockSpec(memory_space=pltpu.VMEM)
ANY = pl.BlockSpec(memory_space=pl.ANY)
F32 = jnp.float32
BF16 = jnp.bfloat16


def params(mebibytes):
    return pltpu.CompilerParams(vmem_limit_bytes=mebibytes << 20)


def cost(flops, transcendentals, data):
    return pl.CostEstimate(
        flops=flops // 16, transcendentals=transcendentals // 16, bytes_accessed=data // 16
    )


def swap(array, axis, mask):
    devices = lax.axis_size(axis)
    return lax.ppermute(array, axis, [(i, i ^ mask) for i in range(devices)])


def swap_both(array, dom_mask, head_mask):
    doms, heads = lax.axis_size("dom"), lax.axis_size("head")
    pairs = [
        (d * heads + h, (d ^ dom_mask) * heads + (h ^ head_mask))
        for d in range(doms)
        for h in range(heads)
    ]
    return lax.ppermute(array, ("dom", "head"), pairs)


def swap_by_core(array, first, second):
    doms, heads = lax.axis_size("dom"), lax.axis_size("head")
    pairs = []
    for d in range(doms):
        for h in range(heads):
            dom_mask, head_mask = second if h % 2 else first
            pairs.append((d * heads + h, (d ^ dom_mask) * heads + (h ^ head_mask)))
    return lax.ppermute(array, ("dom", "head"), pairs)


def dot(a, b):
    return jnp.dot(a, b, preferred_element_type=F32)


def dot_t(a, b):
    return lax.dot_general(a, b, (((1,), (1,)), ((), ())), preferred_element_type=F32)


def same_head(rows, cols, value):
    row = lax.broadcasted_iota(jnp.int32, (rows, cols), 0) // SUBSPACE_WIDTH
    col = lax.broadcasted_iota(jnp.int32, (rows, cols), 1) // SUBSPACE_WIDTH
    return jnp.where(row == col, value, 0.0).astype(BF16)


def head_normed(projected):
    block = same_head(256, 256, 1.0 / SUBSPACE_WIDTH)
    squares = (projected * projected).astype(BF16)
    mean = jnp.concatenate(
        [dot(squares[:, i : i + 256], block) for i in range(0, projected.shape[1], 256)], axis=1
    )
    return projected * lax.rsqrt(mean + norm_eps)


def padded_queries(queries, pair):
    both = queries[:, pair * LANES : (pair + 1) * LANES]
    first = lax.broadcasted_iota(jnp.int32, both.shape, 1) < SUBSPACE_WIDTH
    zero = jnp.zeros_like(both)
    return jnp.concatenate([jnp.where(first, both, zero), jnp.where(first, zero, both)], axis=0)


def attend(queries, keys_ref, values_ref):
    rows = queries.shape[0]
    count = keys_ref.shape[0]
    ones = jnp.ones((count, LANES), BF16)
    numer, denom = [], []
    first = lax.broadcasted_iota(jnp.int32, (rows, LANES), 1) < SUBSPACE_WIDTH
    for pair in range(PAIRS):
        cols = slice(pair * LANES, (pair + 1) * LANES)
        scores = dot_t(padded_queries(queries, pair), keys_ref[:, cols])
        weights = jnp.exp2(scores).astype(BF16)
        sums = dot(weights, jnp.concatenate([values_ref[:, cols], ones], axis=1))
        numer.append(jnp.where(first, sums[:rows, :LANES], sums[rows:, :LANES]))
        denom.append(jnp.where(first, sums[:rows, LANES:], sums[rows:, LANES:]))
    return jnp.concatenate(numer, axis=1), jnp.concatenate(denom, axis=1)


def keys_values(blocks, lookup_ref, content_ref, keys_ref, values_ref):
    nodes = jnp.concatenate(blocks, axis=0)
    keys_ref[...] = head_normed(dot(nodes, lookup_ref[...])).astype(BF16)
    values_ref[...] = dot(nodes, content_ref[...]).astype(BF16)


def lineup_kernel(count, rows, *refs):
    row = 0
    for block in refs[:count]:
        taken = min(block.shape[0], rows - row)
        refs[-1][row : row + taken, :] = block[:taken, :]
        row += taken


def lineup(blocks, after=(), rows=None, work=1 << 15):
    if rows is None:
        rows = sum(block.shape[0] for block in blocks)
    width = blocks[0].shape[1]
    return pl.pallas_call(
        functools.partial(lineup_kernel, len(blocks), rows),
        out_shape=jax.ShapeDtypeStruct((rows, width), BF16),
        in_specs=[VMEM] * len(blocks) + [ANY] * len(after),
        out_specs=VMEM,
        compiler_params=params(4),
        cost_estimate=pl.CostEstimate(flops=0, transcendentals=0, bytes_accessed=work),
        name="lineup",
    )(*blocks, *after)


def rows_kernel(start, block_ref, *refs):
    refs[-1][...] = block_ref[start : start + refs[-1].shape[0], :]


def rows_of(block, start, count, after=()):
    return pl.pallas_call(
        functools.partial(rows_kernel, start),
        out_shape=jax.ShapeDtypeStruct((count, block.shape[1]), BF16),
        in_specs=[VMEM] + [ANY] * len(after),
        out_specs=VMEM,
        compiler_params=params(4),
        cost_estimate=cost(0, 0, 1 << 19),
        name="rows",
    )(block, *after)


def early_kernel(softness_ref, slots_ref, both_ref, side_ref, asking_ref, lookup_ref, content_ref, *refs):
    queries_ref, scale_ref, keys_ref, values_ref, slots_out, temper, sems = refs
    half = both_ref.shape[0] // 2
    copies = [
        pltpu.make_async_copy(softness_ref, temper, sems.at[0]),
        pltpu.make_async_copy(slots_ref, slots_out, sems.at[1]),
    ]
    for copy in copies:
        copy.start()
    nodes = [both_ref[:half, :], side_ref[...]]
    keys_values(nodes, lookup_ref, content_ref, keys_ref, values_ref)
    projected = head_normed(dot(both_ref[...], asking_ref[...]))
    for copy in copies:
        copy.wait()
    width = asking_ref.shape[1]
    head = lax.broadcasted_iota(jnp.int32, (1, width), 1) // SUBSPACE_WIDTH
    scale = jnp.zeros((1, width), F32)
    for h in range(NUM_SUBSPACES):
        scale = jnp.where(head == h, temper[h], scale)
    scale = scale * (math.log2(math.e) / math.sqrt(SUBSPACE_WIDTH))
    scale_ref[...] = scale
    queries = (projected * scale).astype(BF16)
    queries_ref[:half, :] = queries[half:]
    queries_ref[half:, :] = queries[:half]


def early(softness, slots, both, side, asking, lookup, content):
    rows, width = both.shape
    count = rows // 2 + side.shape[0]
    array = lambda n, dtype: jax.ShapeDtypeStruct((n, width), dtype)
    return pl.pallas_call(
        early_kernel,
        out_shape=(array(rows, BF16), array(1, F32), array(count, BF16), array(count, BF16))
        + (jax.ShapeDtypeStruct(slots.shape, jnp.int32),),
        in_specs=[ANY] * 2 + [VMEM] * 5,
        out_specs=(VMEM,) * 5,
        scratch_shapes=[pltpu.SMEM(softness.shape, F32), pltpu.SemaphoreType.DMA((2,))],
        compiler_params=params(16),
        cost_estimate=cost(2 * (rows + 2 * count) * width * width, rows, 4 << 20),
        name="early",
    )(softness, slots, both, side, asking, lookup, content)


def near_kernel(scale_ref, held_keys, held_values, other_ref, first_ref, second_ref, *refs):
    blocks, (asking_ref, lookup_ref, content_ref) = refs[:-8], refs[-8:-5]
    queries_ref, keys_ref, values_ref, numer_ref, denom_ref = refs[-5:]
    held = held_keys.shape[0]
    keys_ref[:held, :] = held_keys[...]
    values_ref[:held, :] = held_values[...]
    nodes = [block[...] for block in blocks]
    keys_values(nodes, lookup_ref, content_ref, keys_ref.at[held:], values_ref.at[held:])
    rows = jnp.concatenate([first_ref[...], second_ref[...], other_ref[...]], axis=0)
    queries = (head_normed(dot(rows, asking_ref[...])) * scale_ref[...]).astype(BF16)
    queries_ref[...] = queries
    numer_ref[...], denom_ref[...] = attend(queries, keys_ref, values_ref)


def near(scale, keys, values, others, blocks, asking, lookup, content):
    rows, width = 2 * others[0].shape[0], others[0].shape[1]
    count = keys.shape[0] + sum(block.shape[0] for block in blocks)
    array = lambda n, dtype: jax.ShapeDtypeStruct((n, width), dtype)
    return pl.pallas_call(
        near_kernel,
        out_shape=(array(rows, BF16),) + (array(count, BF16),) * 2 + (array(rows, F32),) * 2,
        in_specs=[VMEM] * (6 + len(others) + len(blocks)),
        out_specs=(VMEM,) * 5,
        compiler_params=params(16),
        cost_estimate=cost(6 * rows * count * width, rows * count * NUM_SUBSPACES, 4 << 20),
        name="near",
    )(scale, keys, values, *others, *blocks, asking, lookup, content)


def pack(numer, denom):
    lane = lax.broadcasted_iota(jnp.int32, (denom.shape[0], LANES), 1)
    sums = denom[:, :LANES]
    for pair in range(1, PAIRS):
        held = (lane % SUBSPACE_WIDTH) // 16 == pair
        sums = jnp.where(held, denom[:, pair * LANES : (pair + 1) * LANES], sums)
    high = sums.astype(BF16).astype(F32)
    sums = jnp.where(lane % 16 < 8, high, sums - high)
    return jnp.concatenate([numer.astype(BF16), sums.astype(BF16)], axis=1)


def unpack_denom(packed, width):
    lane = lax.broadcasted_iota(jnp.int32, (LANES, width), 0)
    col = lax.broadcasted_iota(jnp.int32, (LANES, width), 1)
    half = (col % LANES) // SUBSPACE_WIDTH
    source = half * SUBSPACE_WIDTH + (col // LANES) * 16
    spread = jnp.where((lane == source) | (lane == source + 8), 1.0, 0.0).astype(BF16)
    return dot(packed, spread)


def denom_rows(denom):
    row = lax.broadcasted_iota(jnp.int32, (PARTS, denom.shape[1]), 0)
    col = lax.broadcasted_iota(jnp.int32, (PARTS, denom.shape[1]), 1)
    high = denom.astype(BF16)
    low = (denom - high.astype(F32)).astype(BF16)
    first = jnp.where(col == row * SUBSPACE_WIDTH, 1.0, 0.0).astype(BF16)
    second = jnp.where(col == (row - NUM_SUBSPACES) * SUBSPACE_WIDTH, 1.0, 0.0).astype(BF16)
    return (dot_t(first, high) + dot_t(second, low)).astype(BF16)


def spread_denom(rows, width):
    row = lax.broadcasted_iota(jnp.int32, (PARTS, width), 0)
    head = lax.broadcasted_iota(jnp.int32, (PARTS, width), 1) // SUBSPACE_WIDTH
    spread = jnp.where(row % NUM_SUBSPACES == head, 1.0, 0.0).astype(BF16)
    return lax.dot_general(
        rows, spread, (((0,), (0,)), ((), ())), preferred_element_type=F32
    )


def call(kernel, steps, parts, wholes, out_parts, out_wholes, scratch, estimate, name, after=()):
    taken = len(parts) + len(wholes)

    def body(*refs):
        kernel(steps, *refs[:taken], *refs[taken + len(after) :])

    if steps == 1:
        grid, part, whole = (), lambda a: VMEM, lambda a: VMEM
    else:
        grid = (steps,)
        part = lambda a: pl.BlockSpec((a.shape[0] // steps,) + a.shape[1:], lambda i: (i, 0))
        whole = lambda a: pl.BlockSpec(a.shape, lambda i: (0, 0))
    return pl.pallas_call(
        body,
        grid=grid,
        out_shape=tuple(out_parts) + tuple(out_wholes),
        in_specs=[part(a) for a in parts] + [whole(a) for a in wholes] + [ANY] * len(after),
        out_specs=tuple(part(a) for a in out_parts) + tuple(whole(a) for a in out_wholes),
        scratch_shapes=scratch,
        compiler_params=params(16),
        cost_estimate=estimate,
        name=name,
    )(*parts, *wholes, *after)


def at_step(steps, step, body):
    if steps == 1:
        body()
    else:
        pl.when(pl.program_id(0) == step)(body)


def far_kernel(steps, *refs):
    blocks, (lookup_ref, content_ref, queries_ref, numer_ref, denom_ref) = refs[:-12], refs[-12:-7]
    keys_ref, values_ref, packed_ref, numer_out, denom_out, numer_sum, denom_sum = refs[-7:]
    pair = numer_ref.shape[0]
    half = pair // 2

    def start():
        numer_sum[...] = numer_ref[...]
        denom_sum[...] = denom_ref[...]

    def end():
        packed_ref[...] = pack(numer_sum[...], denom_sum[...])
        numer_out[...] = numer_sum[half:, :]
        denom_out[...] = denom_sum[half:, :]

    at_step(steps, 0, start)
    nodes = [block[...] for block in blocks]
    keys_values(nodes, lookup_ref, content_ref, keys_ref, values_ref)
    numer, denom = attend(queries_ref[:pair, :], keys_ref, values_ref)
    numer_sum[...] += numer
    denom_sum[...] += denom
    at_step(steps, steps - 1, end)


def far(blocks, block_len, lookup, content, queries, numer, denom):
    rows, width = numer.shape
    half = rows // 2
    count = len(blocks) * blocks[0].shape[0]
    kept = jax.ShapeDtypeStruct((count, width), BF16)
    return call(
        far_kernel,
        blocks[0].shape[0] // block_len,
        blocks,
        (lookup, content, queries, numer, denom),
        (kept, kept),
        (jax.ShapeDtypeStruct((rows, width + LANES), BF16),)
        + (jax.ShapeDtypeStruct((half, width), F32),) * 2,
        [pltpu.VMEM((rows, width), F32)] * 2,
        cost(6 * rows * count * width, rows * count * NUM_SUBSPACES, 4 << 20),
        "far",
    )


def own_first_kernel(queries_ref, keys_ref, values_ref, *refs):
    numer_ref, denom_ref = refs[-2:]
    count = 2 * queries_ref.shape[0]
    numer_ref[...], denom_ref[...] = attend(
        queries_ref[...], keys_ref.at[:count], values_ref.at[:count]
    )


def own_first(queries, keys, values, after):
    rows, width = queries.shape
    return pl.pallas_call(
        own_first_kernel,
        out_shape=(jax.ShapeDtypeStruct((rows, width), F32),) * 2,
        in_specs=[VMEM] * 3 + [ANY] * len(after),
        out_specs=(VMEM,) * 2,
        compiler_params=params(16),
        cost_estimate=cost(8 * rows * rows * width, 2 * rows * rows * NUM_SUBSPACES, 2 << 20),
        name="own_first",
    )(queries, keys, values, *after)


def own_kernel(steps, far_keys, far_values, queries_ref, near_keys, near_values, *refs):
    numer_ref, denom_ref, sent_ref, numer_out, denom_out = refs[:5]
    numer_sum, denom_sum, keys_ref, values_ref = refs[5:]
    rows, width = numer_sum.shape
    half, done, left = rows // 2, 2 * rows, near_keys.shape[0] - 2 * rows

    def start():
        numer_sum[...] = numer_ref[...]
        denom_sum[...] = denom_ref[...]

    def end():
        sent_ref[:half, :] = numer_sum[:half, :].astype(BF16)
        sent_ref[half:, :] = jnp.zeros((PARTS, width), BF16)
        sent_ref[half:, :half] = denom_rows(denom_sum[:half, :])
        numer_out[...] = numer_sum[half:, :]
        denom_out[...] = denom_sum[half:, :]

    at_step(steps, 0, start)
    if left:
        keys_ref[:left, :] = near_keys[done:, :]
        values_ref[:left, :] = near_values[done:, :]
        keys_ref[left:, :] = far_keys[...]
        values_ref[left:, :] = far_values[...]
        numer, denom = attend(queries_ref[...], keys_ref, values_ref)
    else:
        numer, denom = attend(queries_ref[...], far_keys, far_values)
    numer_sum[...] += numer
    denom_sum[...] += denom
    at_step(steps, steps - 1, end)


def own(far_keys, far_values, steps, queries, near_keys, near_values, numer, denom, after):
    rows, width = queries.shape
    half = rows // 2
    count = near_keys.shape[0] - 2 * rows + far_keys.shape[0] // steps
    return call(
        own_kernel,
        steps,
        (far_keys, far_values),
        (queries, near_keys, near_values, numer, denom),
        (),
        (jax.ShapeDtypeStruct((half + PARTS, width), BF16),)
        + (jax.ShapeDtypeStruct((half, width), F32),) * 2,
        [pltpu.VMEM((rows, width), F32)] * 2 + [pltpu.VMEM((count, width), BF16)] * 2,
        cost(4 * rows * count * width, rows * count * NUM_SUBSPACES, 4 << 20),
        "own",
        after,
    )


def combine_kernel(numer_ref, denom_ref, packed_ref, after_ref, packed_out):
    rows, width = numer_ref.shape
    numer = numer_ref[...] + packed_ref[:rows, :width].astype(F32)
    denom = denom_ref[...] + unpack_denom(packed_ref[:rows, width:], width)
    packed_out[...] = pack(numer, denom)


def combine(numer, denom, packed, after):
    return pl.pallas_call(
        combine_kernel,
        out_shape=jax.ShapeDtypeStruct((numer.shape[0], packed.shape[1]), BF16),
        in_specs=[VMEM] * 3 + [ANY],
        out_specs=VMEM,
        compiler_params=params(8),
        cost_estimate=cost(4 * packed.shape[0] * packed.shape[1] * LANES, 0, 1 << 20),
        name="combine",
    )(numer, denom, packed, *after)


def around_kernel(slots_ref, twin_ref, tiles_ref, both_ref, side_ref, across_ref, halo_ref, *refs):
    mine_ref, theirs_ref, slots, sems = refs
    copies = [
        pltpu.make_async_copy(source, slots.at[i], sems.at[i])
        for i, source in enumerate((slots_ref, twin_ref))
    ]
    for copy in copies:
        copy.start()
    group = slots_ref.shape[1] // 3
    me, core = lax.axis_index("head"), lax.axis_index("head") % 2
    part, parts = lax.axis_index("dom"), lax.axis_size("dom")
    beside, beyond = 2 - 2 * (part % 2), 2 * (part % 2)
    inside = (part != 0) & (part != parts - 1)
    pick = lambda first, second: first + core * (second - first)
    order = [(1, 0, True), (pick(beside, 1), pick(0, 2), True), (pick(beside, 1), pick(1, 3), True)]
    order += [(beside, 2, True), (beyond, 0, inside & (core == 0)), (beyond, 1, inside & (core == 0))]
    order += [(beyond, 2, inside)]
    rows = across_ref.shape[0]
    nodes = [both_ref[:rows, :], side_ref[...], across_ref[...], halo_ref[...]]
    for copy in copies:
        copy.wait()
    wide = []
    for receiver in range(2):
        tiles = []
        for side, offset, held in order:
            tile_id = slots[receiver, 0, side * group + (me ^ offset)]
            tile = tiles_ref[jnp.maximum(tile_id, 0)]
            tiles.append(jnp.where((tile_id >= 0) & held, tile, jnp.zeros_like(tile)))
        wide.append(jnp.concatenate(tiles, axis=1))
    sums = dot(jnp.concatenate(wide, axis=0), jnp.concatenate(nodes, axis=0))
    mine_ref[...] = sums[:rows]
    theirs_ref[...] = sums[rows:].astype(BF16)


def around(slots, twin_slots, tiles, blocks, kept, after):
    rows, width = tiles.shape[1], blocks[0].shape[1]

    def body(*refs):
        around_kernel(*refs[:7], *refs[8 + len(after) :])

    return pl.pallas_call(
        body,
        out_shape=(
            jax.ShapeDtypeStruct((rows, width), F32),
            jax.ShapeDtypeStruct((rows, width), BF16),
        ),
        in_specs=[VMEM] * 8 + [ANY] * len(after),
        out_specs=(VMEM,) * 2,
        scratch_shapes=[
            pltpu.SMEM((2,) + slots.shape, jnp.int32),
            pltpu.SemaphoreType.DMA((2,)),
        ],
        compiler_params=params(8),
        cost_estimate=cost(28 * rows * rows * width, 0, 1 << 20),
        name="around",
    )(slots, twin_slots, tiles, *blocks, kept, *after)


def message_kernel(mine_ref, got_ref, inner_ref, outer_ref, gain_ref, local_ref, gain_out):
    gain_out[...] = gain_ref[...]
    aggregate = (mine_ref[...] + got_ref[...].astype(F32)).astype(BF16)
    hidden = jax.nn.gelu(dot(aggregate, inner_ref[...])).astype(BF16)
    local_ref[...] = dot(hidden, outer_ref[...])


def message(mine, got, inner, outer, gain):
    rows, width = mine.shape
    hidden = inner.shape[1]
    return pl.pallas_call(
        message_kernel,
        out_shape=(
            jax.ShapeDtypeStruct((rows, width), F32),
            jax.ShapeDtypeStruct(gain.shape, F32),
        ),
        in_specs=[VMEM] * 5,
        out_specs=(VMEM,) * 2,
        compiler_params=params(16),
        cost_estimate=cost(4 * rows * width * hidden, rows * hidden, 4 << 20),
        name="message",
    )(mine, got, inner, outer, gain)


def finish_kernel(
    numer_ref, denom_ref, crossed_ref, packed_ref, final_ref, gain_ref, local_ref, nodes_ref, out_ref
):
    width = numer_ref.shape[1]
    rows = numer_ref.shape[0]
    numer = numer_ref[...] + crossed_ref[:rows, :].astype(F32) + packed_ref[:, :width].astype(F32)
    denom = denom_ref[...] + spread_denom(crossed_ref[rows:, :rows], width)
    denom += unpack_denom(packed_ref[:, width:], width)
    mixed = (numer / denom).astype(BF16)
    attended = dot(mixed, final_ref[...])
    mean = jnp.mean(attended * attended, axis=-1, keepdims=True)
    normed = attended * lax.rsqrt(mean + norm_eps) * gain_ref[...]
    out_ref[...] = (nodes_ref[...].astype(F32) + local_ref[...] + normed).astype(BF16)


def finish(numer, denom, crossed, packed, final, gain, local, nodes):
    rows, width = nodes.shape
    return pl.pallas_call(
        finish_kernel,
        out_shape=jax.ShapeDtypeStruct((rows, width), BF16),
        in_specs=[VMEM] * 8,
        out_specs=VMEM,
        compiler_params=params(16),
        cost_estimate=cost(2 * rows * width * width, rows, 2 << 20),
        name="finish",
    )(numer, denom, crossed, packed, final, gain, local, nodes)


def shards(
    vertex_embeddings,
    adjacent_group_bank_ids,
    coupling_strength_panels,
    asking_projector,
    lookup_projector,
    content_projector,
    final_projector,
    passing_inner_coefficients,
    passing_outer_coefficients,
    softness_per_subspace,
    mixing_layer_gain,
):
    block_len = vertex_embeddings.shape[0]
    doms = lax.axis_size("dom")
    nodes = vertex_embeddings
    stacked = lambda *arrays: jnp.concatenate(arrays, axis=0)

    distant = swap(nodes, "dom", 4)
    mask = 8
    while mask < doms:
        distant = stacked(distant, swap(stacked(nodes, distant), "dom", mask))
        mask *= 2

    def plane(block):
        side = swap(block, "dom", 1)
        below = swap(block, "head", 2)
        across = swap_both(block, 1, 2)
        return below, side, across

    held = lineup((nodes,))
    twin_slots = swap(adjacent_group_bank_ids.reshape(1, -1), "head", 1)
    both = lineup((held, swap(nodes, "head", 1)))
    side = swap_by_core(both, (1, 0), (0, 2))
    across = swap_by_core(lineup((side,), (), block_len), (0, 2), (1, 0))
    other = swap(nodes, "dom", 2)
    halves = [rows_of(other, at, block_len // 2) for at in (0, block_len // 2)]
    others = (other,) + tuple(swap(part, "head", 1) for part in halves)
    queries, scale, keys, values, slots = early(
        softness_per_subspace,
        adjacent_group_bank_ids.reshape(1, -1),
        both,
        side,
        asking_projector,
        lookup_projector,
        content_projector,
    )
    distant = lineup((distant,), (queries,))
    far_blocks = plane(distant)
    steps = distant.shape[0] // block_len
    if steps == 1:
        near_blocks = (across, distant, far_blocks[1])
        far_blocks = (far_blocks[0], far_blocks[2])
    else:
        near_blocks, far_blocks = (across,), (distant,) + far_blocks
    pair_queries, keys, values, numer, denom = near(
        scale,
        keys,
        values,
        others,
        near_blocks,
        asking_projector,
        lookup_projector,
        content_projector,
    )

    pairs = [(p, p + 2) for p in range(0, doms - 2, 2)] + [(doms - 2, doms - 1)]
    pairs += [(p, p - 2) for p in range(3, doms, 2)] + [(1, 0)]
    halo = lax.ppermute(lineup((side, across), ()), "dom", pairs)
    far_keys, far_values, packed, numer, denom = far(
        far_blocks, block_len, lookup_projector, content_projector, pair_queries, numer, denom
    )
    own_numer, own_denom = own_first(queries, keys, values, (packed,))
    packed = combine(numer, denom, swap(packed, "head", 1), (own_numer,))
    crossed, numer, denom = own(
        far_keys, far_values, steps, queries, keys, values, own_numer, own_denom, (packed,)
    )
    crossed = swap(crossed, "head", 1)
    packed = swap(packed, "dom", 2)
    mine, theirs = around(
        slots,
        twin_slots,
        coupling_strength_panels,
        (both, side, across, halo),
        final_projector,
        (numer,),
    )
    local, gain = message(
        mine,
        swap(theirs, "head", 1),
        passing_inner_coefficients,
        passing_outer_coefficients,
        mixing_layer_gain.reshape(1, -1),
    )
    return finish(
        numer, denom, crossed, packed, final_projector, gain, local, held
    )


def solution(mesh):
    in_specs = (P(("dom", "head"), None), P("dom", "head", None)) + (P(),) * 9
    out_specs = P(("dom", "head"), None)
    return jax.shard_map(shards, mesh=mesh, in_specs=in_specs, out_specs=out_specs, check_vma=False)
```

```python
import functools
import math

import jax
import jax.numpy as jnp
from jax import lax
from jax.experimental import pallas as pl
from jax.experimental.pallas import tpu as pltpu
from jax.sharding import PartitionSpec as P

NUM_SUBSPACES = 8
SUBSPACE_WIDTH = 64
PAIRS = NUM_SUBSPACES // 2
PARTS = 2 * NUM_SUBSPACES
LANES = 128
norm_eps = 1e-06
VMEM = pl.BlockSpec(memory_space=pltpu.VMEM)
ANY = pl.BlockSpec(memory_space=pl.ANY)
F32 = jnp.float32
BF16 = jnp.bfloat16


def params(mebibytes):
    return pltpu.CompilerParams(vmem_limit_bytes=mebibytes << 20)


def cost(flops, transcendentals, data):
    return pl.CostEstimate(
        flops=flops // 16, transcendentals=transcendentals // 16, bytes_accessed=data // 16
    )


def swap(array, axis, mask):
    devices = lax.axis_size(axis)
    return lax.ppermute(array, axis, [(i, i ^ mask) for i in range(devices)])


def swap_both(array, dom_mask, head_mask):
    doms, heads = lax.axis_size("dom"), lax.axis_size("head")
    pairs = [
        (d * heads + h, (d ^ dom_mask) * heads + (h ^ head_mask))
        for d in range(doms)
        for h in range(heads)
    ]
    return lax.ppermute(array, ("dom", "head"), pairs)


def swap_by_core(array, first, second):
    doms, heads = lax.axis_size("dom"), lax.axis_size("head")
    pairs = []
    for d in range(doms):
        for h in range(heads):
            dom_mask, head_mask = second if h % 2 else first
            pairs.append((d * heads + h, (d ^ dom_mask) * heads + (h ^ head_mask)))
    return lax.ppermute(array, ("dom", "head"), pairs)


def dot(a, b):
    return jnp.dot(a, b, preferred_element_type=F32)


def dot_t(a, b):
    return lax.dot_general(a, b, (((1,), (1,)), ((), ())), preferred_element_type=F32)


def same_head(rows, cols, value):
    row = lax.broadcasted_iota(jnp.int32, (rows, cols), 0) // SUBSPACE_WIDTH
    col = lax.broadcasted_iota(jnp.int32, (rows, cols), 1) // SUBSPACE_WIDTH
    return jnp.where(row == col, value, 0.0).astype(BF16)


def head_normed(projected):
    block = same_head(256, 256, 1.0 / SUBSPACE_WIDTH)
    squares = (projected * projected).astype(BF16)
    mean = jnp.concatenate(
        [dot(squares[:, i : i + 256], block) for i in range(0, projected.shape[1], 256)], axis=1
    )
    return projected * lax.rsqrt(mean + norm_eps)


def padded_queries(queries, pair):
    both = queries[:, pair * LANES : (pair + 1) * LANES]
    first = lax.broadcasted_iota(jnp.int32, both.shape, 1) < SUBSPACE_WIDTH
    zero = jnp.zeros_like(both)
    return jnp.concatenate([jnp.where(first, both, zero), jnp.where(first, zero, both)], axis=0)


def attend(queries, keys_ref, values_ref):
    rows = queries.shape[0]
    count = keys_ref.shape[0]
    ones = jnp.ones((count, LANES), BF16)
    numer, denom = [], []
    first = lax.broadcasted_iota(jnp.int32, (rows, LANES), 1) < SUBSPACE_WIDTH
    for pair in range(PAIRS):
        cols = slice(pair * LANES, (pair + 1) * LANES)
        scores = dot_t(padded_queries(queries, pair), keys_ref[:, cols])
        weights = jnp.exp2(scores).astype(BF16)
        sums = dot(weights, jnp.concatenate([values_ref[:, cols], ones], axis=1))
        numer.append(jnp.where(first, sums[:rows, :LANES], sums[rows:, :LANES]))
        denom.append(jnp.where(first, sums[:rows, LANES:], sums[rows:, LANES:]))
    return jnp.concatenate(numer, axis=1), jnp.concatenate(denom, axis=1)


def keys_values(blocks, lookup_ref, content_ref, keys_ref, values_ref):
    nodes = jnp.concatenate(blocks, axis=0)
    keys_ref[...] = head_normed(dot(nodes, lookup_ref[...])).astype(BF16)
    values_ref[...] = dot(nodes, content_ref[...]).astype(BF16)


def lineup_kernel(count, rows, *refs):
    row = 0
    for block in refs[:count]:
        taken = min(block.shape[0], rows - row)
        refs[-1][row : row + taken, :] = block[:taken, :]
        row += taken


def lineup(blocks, after=(), rows=None, work=1 << 15):
    if rows is None:
        rows = sum(block.shape[0] for block in blocks)
    width = blocks[0].shape[1]
    return pl.pallas_call(
        functools.partial(lineup_kernel, len(blocks), rows),
        out_shape=jax.ShapeDtypeStruct((rows, width), BF16),
        in_specs=[VMEM] * len(blocks) + [ANY] * len(after),
        out_specs=VMEM,
        compiler_params=params(4),
        cost_estimate=pl.CostEstimate(flops=0, transcendentals=0, bytes_accessed=work),
        name="lineup",
    )(*blocks, *after)


def rows_kernel(start, block_ref, *refs):
    refs[-1][...] = block_ref[start : start + refs[-1].shape[0], :]


def rows_of(block, start, count, after=()):
    return pl.pallas_call(
        functools.partial(rows_kernel, start),
        out_shape=jax.ShapeDtypeStruct((count, block.shape[1]), BF16),
        in_specs=[VMEM] + [ANY] * len(after),
        out_specs=VMEM,
        compiler_params=params(4),
        cost_estimate=cost(0, 0, 1 << 19),
        name="rows",
    )(block, *after)


def early_kernel(softness_ref, slots_ref, both_ref, side_ref, asking_ref, lookup_ref, content_ref, *refs):
    queries_ref, scale_ref, keys_ref, values_ref, slots_out, temper, sems = refs
    half = both_ref.shape[0] // 2
    copies = [
        pltpu.make_async_copy(softness_ref, temper, sems.at[0]),
        pltpu.make_async_copy(slots_ref, slots_out, sems.at[1]),
    ]
    for copy in copies:
        copy.start()
    nodes = [both_ref[:half, :], side_ref[...]]
    keys_values(nodes, lookup_ref, content_ref, keys_ref, values_ref)
    projected = head_normed(dot(both_ref[...], asking_ref[...]))
    for copy in copies:
        copy.wait()
    width = asking_ref.shape[1]
    head = lax.broadcasted_iota(jnp.int32, (1, width), 1) // SUBSPACE_WIDTH
    scale = jnp.zeros((1, width), F32)
    for h in range(NUM_SUBSPACES):
        scale = jnp.where(head == h, temper[h], scale)
    scale = scale * (math.log2(math.e) / math.sqrt(SUBSPACE_WIDTH))
    scale_ref[...] = scale
    queries = (projected * scale).astype(BF16)
    queries_ref[:half, :] = queries[half:]
    queries_ref[half:, :] = queries[:half]


def early(softness, slots, both, side, asking, lookup, content):
    rows, width = both.shape
    count = rows // 2 + side.shape[0]
    array = lambda n, dtype: jax.ShapeDtypeStruct((n, width), dtype)
    return pl.pallas_call(
        early_kernel,
        out_shape=(array(rows, BF16), array(1, F32), array(count, BF16), array(count, BF16))
        + (jax.ShapeDtypeStruct(slots.shape, jnp.int32),),
        in_specs=[ANY] * 2 + [VMEM] * 5,
        out_specs=(VMEM,) * 5,
        scratch_shapes=[pltpu.SMEM(softness.shape, F32), pltpu.SemaphoreType.DMA((2,))],
        compiler_params=params(16),
        cost_estimate=cost(2 * (rows + 2 * count) * width * width, rows, 4 << 20),
        name="early",
    )(softness, slots, both, side, asking, lookup, content)


def near_kernel(scale_ref, held_keys, held_values, other_ref, first_ref, second_ref, *refs):
    blocks, (asking_ref, lookup_ref, content_ref) = refs[:-8], refs[-8:-5]
    queries_ref, keys_ref, values_ref, numer_ref, denom_ref = refs[-5:]
    held = held_keys.shape[0]
    keys_ref[:held, :] = held_keys[...]
    values_ref[:held, :] = held_values[...]
    nodes = [block[...] for block in blocks]
    keys_values(nodes, lookup_ref, content_ref, keys_ref.at[held:], values_ref.at[held:])
    rows = jnp.concatenate([first_ref[...], second_ref[...], other_ref[...]], axis=0)
    queries = (head_normed(dot(rows, asking_ref[...])) * scale_ref[...]).astype(BF16)
    queries_ref[...] = queries
    numer_ref[...], denom_ref[...] = attend(queries, keys_ref, values_ref)


def near(scale, keys, values, others, blocks, asking, lookup, content):
    rows, width = 2 * others[0].shape[0], others[0].shape[1]
    count = keys.shape[0] + sum(block.shape[0] for block in blocks)
    array = lambda n, dtype: jax.ShapeDtypeStruct((n, width), dtype)
    return pl.pallas_call(
        near_kernel,
        out_shape=(array(rows, BF16),) + (array(count, BF16),) * 2 + (array(rows, F32),) * 2,
        in_specs=[VMEM] * (6 + len(others) + len(blocks)),
        out_specs=(VMEM,) * 5,
        compiler_params=params(16),
        cost_estimate=cost(6 * rows * count * width, rows * count * NUM_SUBSPACES, 4 << 20),
        name="near",
    )(scale, keys, values, *others, *blocks, asking, lookup, content)


def pack(numer, denom):
    lane = lax.broadcasted_iota(jnp.int32, (denom.shape[0], LANES), 1)
    sums = denom[:, :LANES]
    for pair in range(1, PAIRS):
        held = (lane % SUBSPACE_WIDTH) // 16 == pair
        sums = jnp.where(held, denom[:, pair * LANES : (pair + 1) * LANES], sums)
    high = sums.astype(BF16).astype(F32)
    sums = jnp.where(lane % 16 < 8, high, sums - high)
    return jnp.concatenate([numer.astype(BF16), sums.astype(BF16)], axis=1)


def unpack_denom(packed, width):
    lane = lax.broadcasted_iota(jnp.int32, (LANES, width), 0)
    col = lax.broadcasted_iota(jnp.int32, (LANES, width), 1)
    half = (col % LANES) // SUBSPACE_WIDTH
    source = half * SUBSPACE_WIDTH + (col // LANES) * 16
    spread = jnp.where((lane == source) | (lane == source + 8), 1.0, 0.0).astype(BF16)
    return dot(packed, spread)


def denom_rows(denom):
    row = lax.broadcasted_iota(jnp.int32, (PARTS, denom.shape[1]), 0)
    col = lax.broadcasted_iota(jnp.int32, (PARTS, denom.shape[1]), 1)
    high = denom.astype(BF16)
    low = (denom - high.astype(F32)).astype(BF16)
    first = jnp.where(col == row * SUBSPACE_WIDTH, 1.0, 0.0).astype(BF16)
    second = jnp.where(col == (row - NUM_SUBSPACES) * SUBSPACE_WIDTH, 1.0, 0.0).astype(BF16)
    return (dot_t(first, high) + dot_t(second, low)).astype(BF16)


def spread_denom(rows, width):
    row = lax.broadcasted_iota(jnp.int32, (PARTS, width), 0)
    head = lax.broadcasted_iota(jnp.int32, (PARTS, width), 1) // SUBSPACE_WIDTH
    spread = jnp.where(row % NUM_SUBSPACES == head, 1.0, 0.0).astype(BF16)
    return lax.dot_general(
        rows, spread, (((0,), (0,)), ((), ())), preferred_element_type=F32
    )


def call(kernel, steps, parts, wholes, out_parts, out_wholes, scratch, estimate, name, after=()):
    taken = len(parts) + len(wholes)

    def body(*refs):
        kernel(steps, *refs[:taken], *refs[taken + len(after) :])

    if steps == 1:
        grid, part, whole = (), lambda a: VMEM, lambda a: VMEM
    else:
        grid = (steps,)
        part = lambda a: pl.BlockSpec((a.shape[0] // steps,) + a.shape[1:], lambda i: (i, 0))
        whole = lambda a: pl.BlockSpec(a.shape, lambda i: (0, 0))
    return pl.pallas_call(
        body,
        grid=grid,
        out_shape=tuple(out_parts) + tuple(out_wholes),
        in_specs=[part(a) for a in parts] + [whole(a) for a in wholes] + [ANY] * len(after),
        out_specs=tuple(part(a) for a in out_parts) + tuple(whole(a) for a in out_wholes),
        scratch_shapes=scratch,
        compiler_params=params(16),
        cost_estimate=estimate,
        name=name,
    )(*parts, *wholes, *after)


def at_step(steps, step, body):
    if steps == 1:
        body()
    else:
        pl.when(pl.program_id(0) == step)(body)


def far_kernel(steps, *refs):
    blocks, (lookup_ref, content_ref, queries_ref, numer_ref, denom_ref) = refs[:-12], refs[-12:-7]
    keys_ref, values_ref, packed_ref, numer_out, denom_out, numer_sum, denom_sum = refs[-7:]
    pair = numer_ref.shape[0]
    half = pair // 2

    def start():
        numer_sum[...] = numer_ref[...]
        denom_sum[...] = denom_ref[...]

    def end():
        packed_ref[...] = pack(numer_sum[...], denom_sum[...])
        numer_out[...] = numer_sum[half:, :]
        denom_out[...] = denom_sum[half:, :]

    at_step(steps, 0, start)
    nodes = [block[...] for block in blocks]
    keys_values(nodes, lookup_ref, content_ref, keys_ref, values_ref)
    numer, denom = attend(queries_ref[:pair, :], keys_ref, values_ref)
    numer_sum[...] += numer
    denom_sum[...] += denom
    at_step(steps, steps - 1, end)


def far(blocks, block_len, lookup, content, queries, numer, denom):
    rows, width = numer.shape
    half = rows // 2
    count = len(blocks) * blocks[0].shape[0]
    kept = jax.ShapeDtypeStruct((count, width), BF16)
    return call(
        far_kernel,
        blocks[0].shape[0] // block_len,
        blocks,
        (lookup, content, queries, numer, denom),
        (kept, kept),
        (jax.ShapeDtypeStruct((rows, width + LANES), BF16),)
        + (jax.ShapeDtypeStruct((half, width), F32),) * 2,
        [pltpu.VMEM((rows, width), F32)] * 2,
        cost(6 * rows * count * width, rows * count * NUM_SUBSPACES, 4 << 20),
        "far",
    )


def own_first_kernel(queries_ref, keys_ref, values_ref, *refs):
    numer_ref, denom_ref = refs[-2:]
    count = 2 * queries_ref.shape[0]
    numer_ref[...], denom_ref[...] = attend(
        queries_ref[...], keys_ref.at[:count], values_ref.at[:count]
    )


def own_first(queries, keys, values, after):
    rows, width = queries.shape
    return pl.pallas_call(
        own_first_kernel,
        out_shape=(jax.ShapeDtypeStruct((rows, width), F32),) * 2,
        in_specs=[VMEM] * 3 + [ANY] * len(after),
        out_specs=(VMEM,) * 2,
        compiler_params=params(16),
        cost_estimate=cost(8 * rows * rows * width, 2 * rows * rows * NUM_SUBSPACES, 2 << 20),
        name="own_first",
    )(queries, keys, values, *after)


def own_kernel(steps, far_keys, far_values, queries_ref, near_keys, near_values, *refs):
    numer_ref, denom_ref, sent_ref, numer_out, denom_out = refs[:5]
    numer_sum, denom_sum, keys_ref, values_ref = refs[5:]
    rows, width = numer_sum.shape
    half, done, left = rows // 2, 2 * rows, near_keys.shape[0] - 2 * rows

    def start():
        numer_sum[...] = numer_ref[...]
        denom_sum[...] = denom_ref[...]

    def end():
        sent_ref[:half, :] = numer_sum[:half, :].astype(BF16)
        sent_ref[half:, :] = jnp.zeros((PARTS, width), BF16)
        sent_ref[half:, :half] = denom_rows(denom_sum[:half, :])
        numer_out[...] = numer_sum[half:, :]
        denom_out[...] = denom_sum[half:, :]

    at_step(steps, 0, start)
    if left:
        keys_ref[:left, :] = near_keys[done:, :]
        values_ref[:left, :] = near_values[done:, :]
        keys_ref[left:, :] = far_keys[...]
        values_ref[left:, :] = far_values[...]
        numer, denom = attend(queries_ref[...], keys_ref, values_ref)
    else:
        numer, denom = attend(queries_ref[...], far_keys, far_values)
    numer_sum[...] += numer
    denom_sum[...] += denom
    at_step(steps, steps - 1, end)


def own(far_keys, far_values, steps, queries, near_keys, near_values, numer, denom, after):
    rows, width = queries.shape
    half = rows // 2
    count = near_keys.shape[0] - 2 * rows + far_keys.shape[0] // steps
    return call(
        own_kernel,
        steps,
        (far_keys, far_values),
        (queries, near_keys, near_values, numer, denom),
        (),
        (jax.ShapeDtypeStruct((half + PARTS, width), BF16),)
        + (jax.ShapeDtypeStruct((half, width), F32),) * 2,
        [pltpu.VMEM((rows, width), F32)] * 2 + [pltpu.VMEM((count, width), BF16)] * 2,
        cost(4 * rows * count * width, rows * count * NUM_SUBSPACES, 4 << 20),
        "own",
        after,
    )


def combine_kernel(numer_ref, denom_ref, packed_ref, after_ref, packed_out):
    rows, width = numer_ref.shape
    numer = numer_ref[...] + packed_ref[:rows, :width].astype(F32)
    denom = denom_ref[...] + unpack_denom(packed_ref[:rows, width:], width)
    packed_out[...] = pack(numer, denom)


def combine(numer, denom, packed, after):
    return pl.pallas_call(
        combine_kernel,
        out_shape=jax.ShapeDtypeStruct((numer.shape[0], packed.shape[1]), BF16),
        in_specs=[VMEM] * 3 + [ANY],
        out_specs=VMEM,
        compiler_params=params(8),
        cost_estimate=cost(4 * packed.shape[0] * packed.shape[1] * LANES, 0, 1 << 20),
        name="combine",
    )(numer, denom, packed, *after)


def around_kernel(slots_ref, twin_ref, tiles_ref, both_ref, side_ref, across_ref, halo_ref, *refs):
    mine_ref, theirs_ref, slots, sems = refs
    copies = [
        pltpu.make_async_copy(source, slots.at[i], sems.at[i])
        for i, source in enumerate((slots_ref, twin_ref))
    ]
    for copy in copies:
        copy.start()
    group = slots_ref.shape[1] // 3
    me, core = lax.axis_index("head"), lax.axis_index("head") % 2
    part, parts = lax.axis_index("dom"), lax.axis_size("dom")
    beside, beyond = 2 - 2 * (part % 2), 2 * (part % 2)
    inside = (part != 0) & (part != parts - 1)
    pick = lambda first, second: first + core * (second - first)
    order = [(1, 0, True), (beside, 2, True)]
    order += [(pick(beside, 1), pick(0, 2), True), (pick(beside, 1), pick(1, 3), True)]
    order += [(beyond, 0, inside & (core == 0)), (beyond, 1, inside & (core == 0))]
    order += [(beyond, 2, inside)]
    rows = across_ref.shape[0]
    nodes = [
        jnp.concatenate([both_ref[:rows, :], across_ref[...]], axis=0),
        side_ref[...],
        halo_ref[: 2 * rows, :],
        halo_ref[2 * rows :, :],
    ]
    for copy in copies:
        copy.wait()
    columns = []
    for side, offset, held in order:
        tiles = []
        for receiver in range(2):
            tile_id = slots[receiver, 0, side * group + (me ^ offset)]
            tile = tiles_ref[jnp.maximum(tile_id, 0)]
            tiles.append(jnp.where((tile_id >= 0) & held, tile, jnp.zeros_like(tile)))
        columns.append(jnp.concatenate(tiles, axis=0))
    sums = dot(columns[6], nodes[3])
    for i in range(3):
        sums += dot(jnp.concatenate(columns[2 * i : 2 * i + 2], axis=1), nodes[i])
    mine_ref[...] = sums[:rows]
    theirs_ref[...] = sums[rows:].astype(BF16)


def around(slots, twin_slots, tiles, blocks, kept, after):
    rows, width = tiles.shape[1], blocks[0].shape[1]

    def body(*refs):
        around_kernel(*refs[:7], *refs[8 + len(after) :])

    return pl.pallas_call(
        body,
        out_shape=(
            jax.ShapeDtypeStruct((rows, width), F32),
            jax.ShapeDtypeStruct((rows, width), BF16),
        ),
        in_specs=[VMEM] * 8 + [ANY] * len(after),
        out_specs=(VMEM,) * 2,
        scratch_shapes=[
            pltpu.SMEM((2,) + slots.shape, jnp.int32),
            pltpu.SemaphoreType.DMA((2,)),
        ],
        compiler_params=params(8),
        cost_estimate=cost(28 * rows * rows * width, 0, 1 << 20),
        name="around",
    )(slots, twin_slots, tiles, *blocks, kept, *after)


def message_kernel(mine_ref, got_ref, inner_ref, outer_ref, gain_ref, local_ref, gain_out):
    gain_out[...] = gain_ref[...]
    aggregate = (mine_ref[...] + got_ref[...].astype(F32)).astype(BF16)
    hidden = jax.nn.gelu(dot(aggregate, inner_ref[...])).astype(BF16)
    local_ref[...] = dot(hidden, outer_ref[...])


def message(mine, got, inner, outer, gain):
    rows, width = mine.shape
    hidden = inner.shape[1]
    return pl.pallas_call(
        message_kernel,
        out_shape=(
            jax.ShapeDtypeStruct((rows, width), F32),
            jax.ShapeDtypeStruct(gain.shape, F32),
        ),
        in_specs=[VMEM] * 5,
        out_specs=(VMEM,) * 2,
        compiler_params=params(16),
        cost_estimate=cost(4 * rows * width * hidden, rows * hidden, 4 << 20),
        name="message",
    )(mine, got, inner, outer, gain)


def finish_kernel(
    numer_ref, denom_ref, crossed_ref, packed_ref, final_ref, gain_ref, local_ref, nodes_ref, out_ref
):
    width = numer_ref.shape[1]
    rows = numer_ref.shape[0]
    numer = numer_ref[...] + crossed_ref[:rows, :].astype(F32) + packed_ref[:, :width].astype(F32)
    denom = denom_ref[...] + spread_denom(crossed_ref[rows:, :rows], width)
    denom += unpack_denom(packed_ref[:, width:], width)
    mixed = (numer / denom).astype(BF16)
    attended = dot(mixed, final_ref[...])
    mean = jnp.mean(attended * attended, axis=-1, keepdims=True)
    normed = attended * lax.rsqrt(mean + norm_eps) * gain_ref[...]
    out_ref[...] = (nodes_ref[...].astype(F32) + local_ref[...] + normed).astype(BF16)


def finish(numer, denom, crossed, packed, final, gain, local, nodes):
    rows, width = nodes.shape
    return pl.pallas_call(
        finish_kernel,
        out_shape=jax.ShapeDtypeStruct((rows, width), BF16),
        in_specs=[VMEM] * 8,
        out_specs=VMEM,
        compiler_params=params(16),
        cost_estimate=cost(2 * rows * width * width, rows, 2 << 20),
        name="finish",
    )(numer, denom, crossed, packed, final, gain, local, nodes)


def shards(
    vertex_embeddings,
    adjacent_group_bank_ids,
    coupling_strength_panels,
    asking_projector,
    lookup_projector,
    content_projector,
    final_projector,
    passing_inner_coefficients,
    passing_outer_coefficients,
    softness_per_subspace,
    mixing_layer_gain,
):
    block_len = vertex_embeddings.shape[0]
    doms = lax.axis_size("dom")
    nodes = vertex_embeddings
    stacked = lambda *arrays: jnp.concatenate(arrays, axis=0)

    distant = swap(nodes, "dom", 4)
    mask = 8
    while mask < doms:
        distant = stacked(distant, swap(stacked(nodes, distant), "dom", mask))
        mask *= 2

    def plane(block):
        side = swap(block, "dom", 1)
        below = swap(block, "head", 2)
        across = swap_both(block, 1, 2)
        return below, side, across

    held = lineup((nodes,))
    twin_slots = swap(adjacent_group_bank_ids.reshape(1, -1), "head", 1)
    both = lineup((held, swap(nodes, "head", 1)))
    side = swap_by_core(both, (1, 0), (0, 2))
    across = swap_by_core(lineup((side,), (), block_len), (0, 2), (1, 0))
    other = swap(nodes, "dom", 2)
    halves = [rows_of(other, at, block_len // 2) for at in (0, block_len // 2)]
    others = (other,) + tuple(swap(part, "head", 1) for part in halves)
    queries, scale, keys, values, slots = early(
        softness_per_subspace,
        adjacent_group_bank_ids.reshape(1, -1),
        both,
        side,
        asking_projector,
        lookup_projector,
        content_projector,
    )
    distant = lineup((distant,), (queries,))
    far_blocks = plane(distant)
    steps = distant.shape[0] // block_len
    if steps == 1:
        near_blocks = (across, distant, far_blocks[1])
        far_blocks = (far_blocks[0], far_blocks[2])
    else:
        near_blocks, far_blocks = (across,), (distant,) + far_blocks
    pair_queries, keys, values, numer, denom = near(
        scale,
        keys,
        values,
        others,
        near_blocks,
        asking_projector,
        lookup_projector,
        content_projector,
    )

    pairs = [(p, p + 2) for p in range(0, doms - 2, 2)] + [(doms - 2, doms - 1)]
    pairs += [(p, p - 2) for p in range(3, doms, 2)] + [(1, 0)]
    halo = lax.ppermute(lineup((side, across), ()), "dom", pairs)
    far_keys, far_values, packed, numer, denom = far(
        far_blocks, block_len, lookup_projector, content_projector, pair_queries, numer, denom
    )
    own_numer, own_denom = own_first(queries, keys, values, (packed,))
    packed = combine(numer, denom, swap(packed, "head", 1), (own_numer,))
    crossed, numer, denom = own(
        far_keys, far_values, steps, queries, keys, values, own_numer, own_denom, (packed,)
    )
    crossed = swap(crossed, "head", 1)
    packed = swap(packed, "dom", 2)
    mine, theirs = around(
        slots,
        twin_slots,
        coupling_strength_panels,
        (both, side, across, halo),
        final_projector,
        (numer,),
    )
    local, gain = message(
        mine,
        swap(theirs, "head", 1),
        passing_inner_coefficients,
        passing_outer_coefficients,
        mixing_layer_gain.reshape(1, -1),
    )
    return finish(
        numer, denom, crossed, packed, final_projector, gain, local, held
    )


def solution(mesh):
    in_specs = (P(("dom", "head"), None), P("dom", "head", None)) + (P(),) * 9
    out_specs = P(("dom", "head"), None)
    return jax.shard_map(shards, mesh=mesh, in_specs=in_specs, out_specs=out_specs, check_vma=False)
```

```python
import functools
import math

import jax
import jax.numpy as jnp
from jax import lax
from jax.experimental import pallas as pl
from jax.experimental.pallas import tpu as pltpu
from jax.sharding import PartitionSpec as P

NUM_SUBSPACES = 8
SUBSPACE_WIDTH = 64
PAIRS = NUM_SUBSPACES // 2
PARTS = 2 * NUM_SUBSPACES
LANES = 128
norm_eps = 1e-06
VMEM = pl.BlockSpec(memory_space=pltpu.VMEM)
ANY = pl.BlockSpec(memory_space=pl.ANY)
F32 = jnp.float32
BF16 = jnp.bfloat16


def params(mebibytes):
    return pltpu.CompilerParams(vmem_limit_bytes=mebibytes << 20)


def cost(flops, transcendentals, data):
    return pl.CostEstimate(
        flops=flops // 16, transcendentals=transcendentals // 16, bytes_accessed=data // 16
    )


def swap(array, axis, mask):
    devices = lax.axis_size(axis)
    return lax.ppermute(array, axis, [(i, i ^ mask) for i in range(devices)])


def swap_both(array, dom_mask, head_mask):
    doms, heads = lax.axis_size("dom"), lax.axis_size("head")
    pairs = [
        (d * heads + h, (d ^ dom_mask) * heads + (h ^ head_mask))
        for d in range(doms)
        for h in range(heads)
    ]
    return lax.ppermute(array, ("dom", "head"), pairs)


def swap_by_core(array, first, second):
    doms, heads = lax.axis_size("dom"), lax.axis_size("head")
    pairs = []
    for d in range(doms):
        for h in range(heads):
            dom_mask, head_mask = second if h % 2 else first
            pairs.append((d * heads + h, (d ^ dom_mask) * heads + (h ^ head_mask)))
    return lax.ppermute(array, ("dom", "head"), pairs)


def dot(a, b):
    return jnp.dot(a, b, preferred_element_type=F32)


def dot_t(a, b):
    return lax.dot_general(a, b, (((1,), (1,)), ((), ())), preferred_element_type=F32)


def same_head(rows, cols, value):
    row = lax.broadcasted_iota(jnp.int32, (rows, cols), 0) // SUBSPACE_WIDTH
    col = lax.broadcasted_iota(jnp.int32, (rows, cols), 1) // SUBSPACE_WIDTH
    return jnp.where(row == col, value, 0.0).astype(BF16)


def head_normed(projected):
    block = same_head(256, 256, 1.0 / SUBSPACE_WIDTH)
    squares = (projected * projected).astype(BF16)
    mean = jnp.concatenate(
        [dot(squares[:, i : i + 256], block) for i in range(0, projected.shape[1], 256)], axis=1
    )
    return projected * lax.rsqrt(mean + norm_eps)


def padded_queries(queries, pair):
    both = queries[:, pair * LANES : (pair + 1) * LANES]
    first = lax.broadcasted_iota(jnp.int32, both.shape, 1) < SUBSPACE_WIDTH
    zero = jnp.zeros_like(both)
    return jnp.concatenate([jnp.where(first, both, zero), jnp.where(first, zero, both)], axis=0)


def attend(queries, keys_ref, values_ref):
    rows = queries.shape[0]
    count = keys_ref.shape[0]
    ones = jnp.ones((count, LANES), BF16)
    numer, denom = [], []
    first = lax.broadcasted_iota(jnp.int32, (rows, LANES), 1) < SUBSPACE_WIDTH
    for pair in range(PAIRS):
        cols = slice(pair * LANES, (pair + 1) * LANES)
        scores = dot_t(padded_queries(queries, pair), keys_ref[:, cols])
        weights = jnp.exp2(scores).astype(BF16)
        sums = dot(weights, jnp.concatenate([values_ref[:, cols], ones], axis=1))
        numer.append(jnp.where(first, sums[:rows, :LANES], sums[rows:, :LANES]))
        denom.append(jnp.where(first, sums[:rows, LANES:], sums[rows:, LANES:]))
    return jnp.concatenate(numer, axis=1), jnp.concatenate(denom, axis=1)


def keys_values(blocks, lookup_ref, content_ref, keys_ref, values_ref):
    nodes = jnp.concatenate(blocks, axis=0)
    keys_ref[...] = head_normed(dot(nodes, lookup_ref[...])).astype(BF16)
    values_ref[...] = dot(nodes, content_ref[...]).astype(BF16)


def lineup_kernel(count, rows, *refs):
    row = 0
    for block in refs[:count]:
        taken = min(block.shape[0], rows - row)
        refs[-1][row : row + taken, :] = block[:taken, :]
        row += taken


def lineup(blocks, after=(), rows=None, work=1 << 15):
    if rows is None:
        rows = sum(block.shape[0] for block in blocks)
    width = blocks[0].shape[1]
    return pl.pallas_call(
        functools.partial(lineup_kernel, len(blocks), rows),
        out_shape=jax.ShapeDtypeStruct((rows, width), BF16),
        in_specs=[VMEM] * len(blocks) + [ANY] * len(after),
        out_specs=VMEM,
        compiler_params=params(4),
        cost_estimate=pl.CostEstimate(flops=0, transcendentals=0, bytes_accessed=work),
        name="lineup",
    )(*blocks, *after)


def rows_kernel(start, block_ref, *refs):
    refs[-1][...] = block_ref[start : start + refs[-1].shape[0], :]


def rows_of(block, start, count, after=()):
    return pl.pallas_call(
        functools.partial(rows_kernel, start),
        out_shape=jax.ShapeDtypeStruct((count, block.shape[1]), BF16),
        in_specs=[VMEM] + [ANY] * len(after),
        out_specs=VMEM,
        compiler_params=params(4),
        cost_estimate=cost(0, 0, 1 << 19),
        name="rows",
    )(block, *after)


def early_kernel(softness_ref, slots_ref, both_ref, side_ref, asking_ref, lookup_ref, content_ref, *refs):
    queries_ref, scale_ref, keys_ref, values_ref, slots_out, temper, sems = refs
    half = both_ref.shape[0] // 2
    copies = [
        pltpu.make_async_copy(softness_ref, temper, sems.at[0]),
        pltpu.make_async_copy(slots_ref, slots_out, sems.at[1]),
    ]
    for copy in copies:
        copy.start()
    nodes = [both_ref[:half, :], side_ref[...]]
    keys_values(nodes, lookup_ref, content_ref, keys_ref, values_ref)
    projected = head_normed(dot(both_ref[...], asking_ref[...]))
    for copy in copies:
        copy.wait()
    width = asking_ref.shape[1]
    head = lax.broadcasted_iota(jnp.int32, (1, width), 1) // SUBSPACE_WIDTH
    scale = jnp.zeros((1, width), F32)
    for h in range(NUM_SUBSPACES):
        scale = jnp.where(head == h, temper[h], scale)
    scale = scale * (math.log2(math.e) / math.sqrt(SUBSPACE_WIDTH))
    scale_ref[...] = scale
    queries = (projected * scale).astype(BF16)
    queries_ref[:half, :] = queries[half:]
    queries_ref[half:, :] = queries[:half]


def early(softness, slots, both, side, asking, lookup, content):
    rows, width = both.shape
    count = rows // 2 + side.shape[0]
    array = lambda n, dtype: jax.ShapeDtypeStruct((n, width), dtype)
    return pl.pallas_call(
        early_kernel,
        out_shape=(array(rows, BF16), array(1, F32), array(count, BF16), array(count, BF16))
        + (jax.ShapeDtypeStruct(slots.shape, jnp.int32),),
        in_specs=[ANY] * 2 + [VMEM] * 5,
        out_specs=(VMEM,) * 5,
        scratch_shapes=[pltpu.SMEM(softness.shape, F32), pltpu.SemaphoreType.DMA((2,))],
        compiler_params=params(16),
        cost_estimate=cost(2 * (rows + 2 * count) * width * width, rows, 4 << 20),
        name="early",
    )(softness, slots, both, side, asking, lookup, content)


def near_kernel(scale_ref, held_keys, held_values, other_ref, first_ref, second_ref, *refs):
    blocks, (asking_ref, lookup_ref, content_ref) = refs[:-8], refs[-8:-5]
    queries_ref, keys_ref, values_ref, numer_ref, denom_ref = refs[-5:]
    held = held_keys.shape[0]
    keys_ref[:held, :] = held_keys[...]
    values_ref[:held, :] = held_values[...]
    nodes = [block[...] for block in blocks]
    keys_values(nodes, lookup_ref, content_ref, keys_ref.at[held:], values_ref.at[held:])
    rows = jnp.concatenate([first_ref[...], second_ref[...], other_ref[...]], axis=0)
    queries = (head_normed(dot(rows, asking_ref[...])) * scale_ref[...]).astype(BF16)
    queries_ref[...] = queries
    numer_ref[...], denom_ref[...] = attend(queries, keys_ref, values_ref)


def near(scale, keys, values, others, blocks, asking, lookup, content):
    rows, width = 2 * others[0].shape[0], others[0].shape[1]
    count = keys.shape[0] + sum(block.shape[0] for block in blocks)
    array = lambda n, dtype: jax.ShapeDtypeStruct((n, width), dtype)
    return pl.pallas_call(
        near_kernel,
        out_shape=(array(rows, BF16),) + (array(count, BF16),) * 2 + (array(rows, F32),) * 2,
        in_specs=[VMEM] * (6 + len(others) + len(blocks)),
        out_specs=(VMEM,) * 5,
        compiler_params=params(16),
        cost_estimate=cost(6 * rows * count * width, rows * count * NUM_SUBSPACES, 4 << 20),
        name="near",
    )(scale, keys, values, *others, *blocks, asking, lookup, content)


def pack(numer, denom):
    lane = lax.broadcasted_iota(jnp.int32, (denom.shape[0], LANES), 1)
    sums = denom[:, :LANES]
    for pair in range(1, PAIRS):
        held = (lane % SUBSPACE_WIDTH) // 16 == pair
        sums = jnp.where(held, denom[:, pair * LANES : (pair + 1) * LANES], sums)
    high = sums.astype(BF16).astype(F32)
    sums = jnp.where(lane % 16 < 8, high, sums - high)
    return jnp.concatenate([numer.astype(BF16), sums.astype(BF16)], axis=1)


def unpack_denom(packed, width):
    lane = lax.broadcasted_iota(jnp.int32, (LANES, width), 0)
    col = lax.broadcasted_iota(jnp.int32, (LANES, width), 1)
    half = (col % LANES) // SUBSPACE_WIDTH
    source = half * SUBSPACE_WIDTH + (col // LANES) * 16
    spread = jnp.where((lane == source) | (lane == source + 8), 1.0, 0.0).astype(BF16)
    return dot(packed, spread)


def denom_rows(denom):
    row = lax.broadcasted_iota(jnp.int32, (PARTS, denom.shape[1]), 0)
    col = lax.broadcasted_iota(jnp.int32, (PARTS, denom.shape[1]), 1)
    high = denom.astype(BF16)
    low = (denom - high.astype(F32)).astype(BF16)
    first = jnp.where(col == row * SUBSPACE_WIDTH, 1.0, 0.0).astype(BF16)
    second = jnp.where(col == (row - NUM_SUBSPACES) * SUBSPACE_WIDTH, 1.0, 0.0).astype(BF16)
    return (dot_t(first, high) + dot_t(second, low)).astype(BF16)


def spread_denom(rows, width):
    row = lax.broadcasted_iota(jnp.int32, (PARTS, width), 0)
    head = lax.broadcasted_iota(jnp.int32, (PARTS, width), 1) // SUBSPACE_WIDTH
    spread = jnp.where(row % NUM_SUBSPACES == head, 1.0, 0.0).astype(BF16)
    return lax.dot_general(
        rows, spread, (((0,), (0,)), ((), ())), preferred_element_type=F32
    )


def call(kernel, steps, parts, wholes, out_parts, out_wholes, scratch, estimate, name, after=()):
    taken = len(parts) + len(wholes)

    def body(*refs):
        kernel(steps, *refs[:taken], *refs[taken + len(after) :])

    if steps == 1:
        grid, part, whole = (), lambda a: VMEM, lambda a: VMEM
    else:
        grid = (steps,)
        part = lambda a: pl.BlockSpec((a.shape[0] // steps,) + a.shape[1:], lambda i: (i, 0))
        whole = lambda a: pl.BlockSpec(a.shape, lambda i: (0, 0))
    return pl.pallas_call(
        body,
        grid=grid,
        out_shape=tuple(out_parts) + tuple(out_wholes),
        in_specs=[part(a) for a in parts] + [whole(a) for a in wholes] + [ANY] * len(after),
        out_specs=tuple(part(a) for a in out_parts) + tuple(whole(a) for a in out_wholes),
        scratch_shapes=scratch,
        compiler_params=params(16),
        cost_estimate=estimate,
        name=name,
    )(*parts, *wholes, *after)


def at_step(steps, step, body):
    if steps == 1:
        body()
    else:
        pl.when(pl.program_id(0) == step)(body)


def far_kernel(steps, *refs):
    blocks, (lookup_ref, content_ref, queries_ref, numer_ref, denom_ref) = refs[:-12], refs[-12:-7]
    keys_ref, values_ref, packed_ref, numer_out, denom_out, numer_sum, denom_sum = refs[-7:]
    pair = numer_ref.shape[0]
    half = pair // 2

    def start():
        numer_sum[...] = numer_ref[...]
        denom_sum[...] = denom_ref[...]

    def end():
        packed_ref[...] = pack(numer_sum[...], denom_sum[...])
        numer_out[...] = numer_sum[half:, :]
        denom_out[...] = denom_sum[half:, :]

    at_step(steps, 0, start)
    nodes = [block[...] for block in blocks]
    keys_values(nodes, lookup_ref, content_ref, keys_ref, values_ref)
    numer, denom = attend(queries_ref[:pair, :], keys_ref, values_ref)
    numer_sum[...] += numer
    denom_sum[...] += denom
    at_step(steps, steps - 1, end)


def far(blocks, block_len, lookup, content, queries, numer, denom):
    rows, width = numer.shape
    half = rows // 2
    count = len(blocks) * blocks[0].shape[0]
    kept = jax.ShapeDtypeStruct((count, width), BF16)
    return call(
        far_kernel,
        blocks[0].shape[0] // block_len,
        blocks,
        (lookup, content, queries, numer, denom),
        (kept, kept),
        (jax.ShapeDtypeStruct((rows, width + LANES), BF16),)
        + (jax.ShapeDtypeStruct((half, width), F32),) * 2,
        [pltpu.VMEM((rows, width), F32)] * 2,
        cost(6 * rows * count * width, rows * count * NUM_SUBSPACES, 4 << 20),
        "far",
    )


def own_first_kernel(queries_ref, keys_ref, values_ref, *refs):
    numer_ref, denom_ref = refs[-2:]
    count = 2 * queries_ref.shape[0]
    numer_ref[...], denom_ref[...] = attend(
        queries_ref[...], keys_ref.at[:count], values_ref.at[:count]
    )


def own_first(queries, keys, values, after):
    rows, width = queries.shape
    return pl.pallas_call(
        own_first_kernel,
        out_shape=(jax.ShapeDtypeStruct((rows, width), F32),) * 2,
        in_specs=[VMEM] * 3 + [ANY] * len(after),
        out_specs=(VMEM,) * 2,
        compiler_params=params(16),
        cost_estimate=cost(8 * rows * rows * width, 2 * rows * rows * NUM_SUBSPACES, 2 << 20),
        name="own_first",
    )(queries, keys, values, *after)


def own_kernel(steps, far_keys, far_values, queries_ref, near_keys, near_values, *refs):
    numer_ref, denom_ref, sent_ref, numer_out, denom_out = refs[:5]
    numer_sum, denom_sum, keys_ref, values_ref = refs[5:]
    rows, width = numer_sum.shape
    half, done, left = rows // 2, 2 * rows, near_keys.shape[0] - 2 * rows

    def start():
        numer_sum[...] = numer_ref[...]
        denom_sum[...] = denom_ref[...]

    def end():
        sent_ref[:half, :] = numer_sum[:half, :].astype(BF16)
        sent_ref[half:, :] = jnp.zeros((PARTS, width), BF16)
        sent_ref[half:, :half] = denom_rows(denom_sum[:half, :])
        numer_out[...] = numer_sum[half:, :]
        denom_out[...] = denom_sum[half:, :]

    at_step(steps, 0, start)
    if left:
        keys_ref[:left, :] = near_keys[done:, :]
        values_ref[:left, :] = near_values[done:, :]
        keys_ref[left:, :] = far_keys[...]
        values_ref[left:, :] = far_values[...]
        numer, denom = attend(queries_ref[...], keys_ref, values_ref)
    else:
        numer, denom = attend(queries_ref[...], far_keys, far_values)
    numer_sum[...] += numer
    denom_sum[...] += denom
    at_step(steps, steps - 1, end)


def own(far_keys, far_values, steps, queries, near_keys, near_values, numer, denom, after):
    rows, width = queries.shape
    half = rows // 2
    count = near_keys.shape[0] - 2 * rows + far_keys.shape[0] // steps
    return call(
        own_kernel,
        steps,
        (far_keys, far_values),
        (queries, near_keys, near_values, numer, denom),
        (),
        (jax.ShapeDtypeStruct((half + PARTS, width), BF16),)
        + (jax.ShapeDtypeStruct((half, width), F32),) * 2,
        [pltpu.VMEM((rows, width), F32)] * 2 + [pltpu.VMEM((count, width), BF16)] * 2,
        cost(4 * rows * count * width, rows * count * NUM_SUBSPACES, 4 << 20),
        "own",
        after,
    )


def combine_kernel(numer_ref, denom_ref, packed_ref, after_ref, packed_out):
    rows, width = numer_ref.shape
    numer = numer_ref[...] + packed_ref[:rows, :width].astype(F32)
    denom = denom_ref[...] + unpack_denom(packed_ref[:rows, width:], width)
    packed_out[...] = pack(numer, denom)


def combine(numer, denom, packed, after):
    return pl.pallas_call(
        combine_kernel,
        out_shape=jax.ShapeDtypeStruct((numer.shape[0], packed.shape[1]), BF16),
        in_specs=[VMEM] * 3 + [ANY],
        out_specs=VMEM,
        compiler_params=params(8),
        cost_estimate=cost(4 * packed.shape[0] * packed.shape[1] * LANES, 0, 1 << 20),
        name="combine",
    )(numer, denom, packed, *after)


def around_kernel(slots_ref, twin_ref, tiles_ref, both_ref, side_ref, across_ref, halo_ref, *refs):
    mine_ref, theirs_ref, slots, sems = refs
    copies = [
        pltpu.make_async_copy(source, slots.at[i], sems.at[i])
        for i, source in enumerate((slots_ref, twin_ref))
    ]
    for copy in copies:
        copy.start()
    group = slots_ref.shape[1] // 3
    me, core = lax.axis_index("head"), lax.axis_index("head") % 2
    part, parts = lax.axis_index("dom"), lax.axis_size("dom")
    beside, beyond = 2 - 2 * (part % 2), 2 * (part % 2)
    inside = (part != 0) & (part != parts - 1)
    pick = lambda first, second: first + core * (second - first)
    order = [(1, 0, True), (pick(beside, 1), pick(0, 2), True), (pick(beside, 1), pick(1, 3), True)]
    order += [(beside, 2, True), (beyond, 0, inside & (core == 0)), (beyond, 1, inside & (core == 0))]
    order += [(beyond, 2, inside)]
    rows = across_ref.shape[0]
    nodes = [both_ref[:rows, :], side_ref[...], across_ref[...], halo_ref[...]]
    for copy in copies:
        copy.wait()
    wide = []
    for receiver in range(2):
        tiles = []
        for side, offset, held in order:
            tile_id = slots[receiver, 0, side * group + (me ^ offset)]
            tile = tiles_ref[jnp.maximum(tile_id, 0)]
            tiles.append(jnp.where((tile_id >= 0) & held, tile, jnp.zeros_like(tile)))
        wide.append(jnp.concatenate(tiles, axis=1))
    sums = dot(jnp.concatenate(wide, axis=0), jnp.concatenate(nodes, axis=0))
    mine_ref[...] = sums[:rows]
    theirs_ref[...] = sums[rows:].astype(BF16)


def around(slots, twin_slots, tiles, blocks, kept, after):
    rows, width = tiles.shape[1], blocks[0].shape[1]

    def body(*refs):
        around_kernel(*refs[:7], *refs[8 + len(after) :])

    return pl.pallas_call(
        body,
        out_shape=(
            jax.ShapeDtypeStruct((rows, width), F32),
            jax.ShapeDtypeStruct((rows, width), BF16),
        ),
        in_specs=[VMEM] * 8 + [ANY] * len(after),
        out_specs=(VMEM,) * 2,
        scratch_shapes=[
            pltpu.SMEM((2,) + slots.shape, jnp.int32),
            pltpu.SemaphoreType.DMA((2,)),
        ],
        compiler_params=params(8),
        cost_estimate=cost(28 * rows * rows * width, 0, 1 << 20),
        name="around",
    )(slots, twin_slots, tiles, *blocks, kept, *after)


def message_kernel(mine_ref, got_ref, inner_ref, outer_ref, gain_ref, local_ref, gain_out):
    gain_out[...] = gain_ref[...]
    aggregate = (mine_ref[...] + got_ref[...].astype(F32)).astype(BF16)
    hidden = jax.nn.gelu(dot(aggregate, inner_ref[...])).astype(BF16)
    local_ref[...] = dot(hidden, outer_ref[...])


def message(mine, got, inner, outer, gain):
    rows, width = mine.shape
    hidden = inner.shape[1]
    return pl.pallas_call(
        message_kernel,
        out_shape=(
            jax.ShapeDtypeStruct((rows, width), F32),
            jax.ShapeDtypeStruct(gain.shape, F32),
        ),
        in_specs=[VMEM] * 5,
        out_specs=(VMEM,) * 2,
        compiler_params=params(16),
        cost_estimate=cost(4 * rows * width * hidden, rows * hidden, 4 << 20),
        name="message",
    )(mine, got, inner, outer, gain)


def finish_kernel(
    numer_ref, denom_ref, crossed_ref, packed_ref, final_ref, gain_ref, local_ref, nodes_ref, out_ref,
    held, sems,
):
    width = numer_ref.shape[1]
    rows = numer_ref.shape[0]
    numer = numer_ref[...] + crossed_ref[:rows, :].astype(F32) + packed_ref[:, :width].astype(F32)
    denom = denom_ref[...] + spread_denom(crossed_ref[rows:, :rows], width)
    denom += unpack_denom(packed_ref[:, width:], width)
    mixed = (numer / denom).astype(BF16)
    attended = dot(mixed, final_ref[...])
    half = rows // 2
    copies = []
    for at in range(2):
        part = slice(at * half, (at + 1) * half)
        here = attended[part]
        mean = jnp.mean(here * here, axis=-1, keepdims=True)
        normed = here * lax.rsqrt(mean + norm_eps) * gain_ref[...]
        total = nodes_ref[part, :].astype(F32) + local_ref[part, :] + normed
        held[at] = total.astype(BF16)
        copy = pltpu.make_async_copy(held.at[at], out_ref.at[pl.ds(at * half, half)], sems.at[at])
        copy.start()
        copies.append(copy)
    for copy in copies:
        copy.wait()


def finish(numer, denom, crossed, packed, final, gain, local, nodes):
    rows, width = nodes.shape
    return pl.pallas_call(
        finish_kernel,
        out_shape=jax.ShapeDtypeStruct((rows, width), BF16),
        in_specs=[VMEM] * 8,
        out_specs=ANY,
        scratch_shapes=[
            pltpu.VMEM((2, rows // 2, width), BF16),
            pltpu.SemaphoreType.DMA((2,)),
        ],
        compiler_params=params(16),
        cost_estimate=cost(2 * rows * width * width, rows, 2 << 20),
        name="finish",
    )(numer, denom, crossed, packed, final, gain, local, nodes)


def shards(
    vertex_embeddings,
    adjacent_group_bank_ids,
    coupling_strength_panels,
    asking_projector,
    lookup_projector,
    content_projector,
    final_projector,
    passing_inner_coefficients,
    passing_outer_coefficients,
    softness_per_subspace,
    mixing_layer_gain,
):
    block_len = vertex_embeddings.shape[0]
    doms = lax.axis_size("dom")
    nodes = vertex_embeddings
    stacked = lambda *arrays: jnp.concatenate(arrays, axis=0)

    distant = swap(nodes, "dom", 4)
    mask = 8
    while mask < doms:
        distant = stacked(distant, swap(stacked(nodes, distant), "dom", mask))
        mask *= 2

    def plane(block):
        side = swap(block, "dom", 1)
        below = swap(block, "head", 2)
        across = swap_both(block, 1, 2)
        return below, side, across

    held = lineup((nodes,))
    twin_slots = swap(adjacent_group_bank_ids.reshape(1, -1), "head", 1)
    both = lineup((held, swap(nodes, "head", 1)))
    side = swap_by_core(both, (1, 0), (0, 2))
    across = swap_by_core(lineup((side,), (), block_len), (0, 2), (1, 0))
    other = swap(nodes, "dom", 2)
    halves = [rows_of(other, at, block_len // 2) for at in (0, block_len // 2)]
    others = (other,) + tuple(swap(part, "head", 1) for part in halves)
    queries, scale, keys, values, slots = early(
        softness_per_subspace,
        adjacent_group_bank_ids.reshape(1, -1),
        both,
        side,
        asking_projector,
        lookup_projector,
        content_projector,
    )
    distant = lineup((distant,), (queries,))
    far_blocks = plane(distant)
    steps = distant.shape[0] // block_len
    if steps == 1:
        near_blocks = (across, distant, far_blocks[1])
        far_blocks = (far_blocks[0], far_blocks[2])
    else:
        near_blocks, far_blocks = (across,), (distant,) + far_blocks
    pair_queries, keys, values, numer, denom = near(
        scale,
        keys,
        values,
        others,
        near_blocks,
        asking_projector,
        lookup_projector,
        content_projector,
    )

    pairs = [(p, p + 2) for p in range(0, doms - 2, 2)] + [(doms - 2, doms - 1)]
    pairs += [(p, p - 2) for p in range(3, doms, 2)] + [(1, 0)]
    halo = lax.ppermute(lineup((side, across), ()), "dom", pairs)
    far_keys, far_values, packed, numer, denom = far(
        far_blocks, block_len, lookup_projector, content_projector, pair_queries, numer, denom
    )
    own_numer, own_denom = own_first(queries, keys, values, (packed,))
    packed = combine(numer, denom, swap(packed, "head", 1), (own_numer,))
    crossed, numer, denom = own(
        far_keys, far_values, steps, queries, keys, values, own_numer, own_denom, (packed,)
    )
    crossed = swap(crossed, "head", 1)
    packed = swap(packed, "dom", 2)
    mine, theirs = around(
        slots,
        twin_slots,
        coupling_strength_panels,
        (both, side, across, halo),
        final_projector,
        (numer,),
    )
    local, gain = message(
        mine,
        swap(theirs, "head", 1),
        passing_inner_coefficients,
        passing_outer_coefficients,
        mixing_layer_gain.reshape(1, -1),
    )
    return finish(
        numer, denom, crossed, packed, final_projector, gain, local, held
    )


def solution(mesh):
    in_specs = (P(("dom", "head"), None), P("dom", "head", None)) + (P(),) * 9
    out_specs = P(("dom", "head"), None)
    return jax.shard_map(shards, mesh=mesh, in_specs=in_specs, out_specs=out_specs, check_vma=False)
```
